512 devices in a mesh: angle: 64 (over y, z), cuts: 8 (over x, core).
Axes of the slice: x: 4, y: 8, z: 8, core: 2. Of those that a mesh axis runs over, the one named last changes fastest.
Arguments:
- sinogram: bfloat16 [8, 768, 4096], P('cuts', 'angle'), may hold values from -6 to 6
- estimate: bfloat16 [8, 128, 4096], P('cuts', 'angle'), may hold values from -6 to 6
- interp_bank: float32 [4, 128, 64], replicated, may hold values from -0.05 to 0.95
- interp_index: int32 [128], replicated, may hold values from 0 to 3
- slice_taps: float32 [3], replicated, may hold values from 0.3 to 1
Outputs:
- updated: float32 [8, 128, 4096], P('cuts', 'angle')
The draws below stay inside these ranges and needn't reach their ends.
Inputs may be any that keep to these rules, and one draw needn't show every extreme that they name: `interp_index`: entries 0 and 1 are not read.
All inputs are finite; a program needn't handle non-finite values.
Results may differ from the reference program's by a relative error of at most 0.0003.
Values sent between devices are 32-bit elements; how exact they have to be, the bound alone decides.
A program may use at most 64 MiB of HBM per device.

```python
import math
import jax
import jax.numpy as jnp
from jax import lax

COLS = 4096
VIEWS_DEV = 12
LEAF_ROWS = 2
KINDS = 4
GROUPS = 64
SLICES = 8
VIEWS = 768
ROWS = 128
LEVELS = 6


def draw_interp_bank(key, part):
    key = jax.random.fold_in(key, 7)
    key_main, key_side, key_noise = jax.random.split(key, 3)
    row_ids = jnp.arange(ROWS, dtype=jnp.int32)[:, None]
    col_ids = jnp.arange(ROWS // 2, dtype=jnp.int32)[None, :]
    main_mask = col_ids == row_ids // 2
    side_mask = col_ids == row_ids // 2 + 2 * (row_ids % 2) - 1
    main_weight = jax.random.uniform(key_main, (KINDS, ROWS, 1), jnp.float32, 0.5, 0.9)
    side_weight = jax.random.uniform(key_side, (KINDS, ROWS, 1), jnp.float32, 0.15, 0.35)
    noise = jnp.clip(0.01 * jax.random.normal(key_noise, (KINDS, ROWS, ROWS // 2), jnp.float32), -0.04, 0.04)
    bank = jnp.where(main_mask[None], main_weight, 0.0) + jnp.where(side_mask[None], side_weight, 0.0) + noise
    return bank.astype(jnp.float32)


def place_ends(array, stream_key, low, top_value):
    shape = array.shape
    index_at = [jax.random.randint(jax.random.fold_in(stream_key, axis), (), 0, shape[axis]) for axis in range(len(shape))]
    array = array.at[tuple(index_at)].set(low)
    longest = shape.index(max(shape))
    index_at[longest] = (index_at[longest] + 1) % shape[longest]
    return array.at[tuple(index_at)].set(top_value)


def steps_of(own_key, shape, pieces, low, largest):
    level = 1.0
    for position, shards_of in pieces:
        steps = jax.random.uniform(jax.random.fold_in(jax.random.fold_in(own_key, 6), position), (shards_of,), jnp.float32, low / len(pieces), largest / len(pieces))
        level = level * jnp.repeat(jnp.exp(steps), shape[position] // shards_of).reshape((-1,) + (1,) * (len(shape) - 1 - position))
    return level


def centred(rng, extent, deviation, limit, pieces=(), kind=jnp.bfloat16):
    factor_of = steps_of(rng, extent, pieces, -0.22, 0.18) if pieces else 1.0
    result = jax.random.normal(rng, extent, jnp.float32) * deviation * factor_of
    return jnp.minimum(jnp.maximum(result, -limit), limit).astype(kind)


def setup_inputs(seed: int = 0) -> dict:
    key_list = jax.random.split(jax.random.key(seed), 6)
    return {
        "sinogram": centred(key_list[0], (SLICES, VIEWS, COLS), 1.0, 6.0, ((0, 8), (1, 64))),
        "estimate": centred(key_list[1], (SLICES, ROWS, COLS), 1.0, 6.0, ((0, 8), (1, 64))),
        "interp_bank": draw_interp_bank(jax.random.fold_in(key_list[5], 71), 0),
        "interp_index": place_ends(jax.random.randint(key_list[3], (2 * GROUPS,), 0, KINDS), jax.random.fold_in(key_list[3], 1), 0, KINDS - 1).astype(jnp.int32),
        "slice_taps": jnp.clip(jax.random.uniform(key_list[4], (3,), jnp.float32, 0.3, 1.0), 0.3, 1.0),
    }


def leaf_image(sino_group, group_id, group_count, leaf_rows):
    view_count, columns = sino_group.shape
    views_total = view_count * group_count
    row_ids = jnp.arange(leaf_rows, dtype=jnp.int32)[:, None, None]
    view_ids = group_id * view_count + jnp.arange(view_count, dtype=jnp.int32)[None, :, None]
    col_ids = jnp.arange(columns, dtype=jnp.int32)[None, None, :]
    shifts = (2 * row_ids + 1 - leaf_rows) * (2 * view_ids + 1 - views_total) * group_count // (4 * views_total)
    source = col_ids - shifts
    inside = (source >= 0) & (source < columns)
    spread = jnp.broadcast_to(sino_group.astype(jnp.float32)[None], (leaf_rows, view_count, columns))
    picked = jnp.take_along_axis(spread, jnp.clip(source, 0, columns - 1), axis=2)
    summed = lax.optimization_barrier(jnp.sum(jnp.where(inside, picked, jnp.float32(0.0)), axis=1))
    return summed * (1.0 / math.sqrt(view_count))

def reference(sinogram, estimate, interp_bank, interp_index, slice_taps):

    def one_slice(sino_slice):
        grouped = sino_slice.reshape(GROUPS, VIEWS_DEV, COLS)
        group_ids = jnp.arange(GROUPS, dtype=jnp.int32)
        images = lax.map(lambda pair_args: leaf_image(pair_args[0], pair_args[1], GROUPS, LEAF_ROWS), (grouped, group_ids))
        for tree_level in range(LEVELS):
            node_count = GROUPS >> tree_level
            sub_rows = LEAF_ROWS << tree_level
            heap_ids = node_count + jnp.arange(node_count, dtype=jnp.int32)
            matrices = interp_bank[:, :2 * sub_rows, :sub_rows][interp_index[heap_ids]]
            refined = jnp.einsum('nij,njc->nic', matrices, images, precision=lax.Precision.HIGHEST)
            images = refined.reshape(node_count // 2, 2, 2 * sub_rows, COLS).sum(axis=1)
        return images[0]
    projected = lax.map(one_slice, sinogram)
    empty_slice = jnp.zeros((1, ROWS, COLS), jnp.float32)
    lower_slice = jnp.concatenate([empty_slice, projected[:-1]], axis=0)
    upper_slice = jnp.concatenate([projected[1:], empty_slice], axis=0)
    mixed = slice_taps[0] * lower_slice + slice_taps[1] * projected + slice_taps[2] * upper_slice
    return estimate.astype(jnp.float32) - mixed
```

```python
import functools
import math

import jax
import jax.numpy as jnp
from jax import lax
from jax.experimental import pallas as pl
from jax.experimental.pallas import tpu as pltpu
from jax.sharding import PartitionSpec as P

MESH = pl.DeviceIdType.MESH
SIDE = 8
LANES = 128
OWNERS = ((0, 0), (1, 0), (2, 0), (3, 0), (4, 0), (5, 0), (6, 0), (7, 0))
BLOCKS = len(OWNERS)


def parts_of(value):
    high = value.astype(jnp.bfloat16)
    low = (value - high.astype(jnp.float32)).astype(jnp.bfloat16)
    return high, low


def tree_matrix(bank_ref, index_ref, levels, size):
    iota = lambda shape, dim: lax.broadcasted_iota(jnp.int32, shape, dim)
    kinds, half = bank_ref.shape[:2]
    index = jnp.broadcast_to(index_ref[...].astype(jnp.float32), (8, size))
    product = None
    for level in range(1, levels + 1):
        width = size >> level
        row, col = iota((size, size), 0), iota((size, size), 1)
        chosen = (row == (1 << level) + col // width).astype(jnp.float32)
        kind = jnp.dot(index, chosen, preferred_element_type=jnp.float32)[0:1]
        block = jnp.zeros((2 * width, size), jnp.float32)
        pick = iota((half, size), 0) == iota((half, size), 1) % width
        for k in range(kinds):
            place = jnp.where(pick & (jnp.abs(kind - k) < 0.5), 1.0, 0.0)
            block += lax.dot_general(
                bank_ref[k, :, :],
                place,
                (((0,), (0,)), ((), ())),
                precision=lax.Precision.HIGHEST,
                preferred_element_type=jnp.float32,
            )[: 2 * width]
        if 2 * width < 8:
            block = jnp.concatenate([block] * (8 // (2 * width)), axis=0)
        factor = jnp.concatenate([block] * (size // block.shape[0]), axis=0)
        factor = jnp.where(row // (2 * width) == col // (2 * width), factor, 0.0)
        if product is None:
            product = factor
        else:
            product = jnp.dot(
                product, factor, precision=lax.Precision.HIGHEST, preferred_element_type=jnp.float32
            )
    return product


def kernel(
    sino_any, bank_any, index_any, taps_any, out_ref,
    sino_ref, bank_ref, index_ref, taps_ref, send_buf, leaf_buf, result_buf, image_buf, tree_buf,
    local_sem, leaf_send, leaf_recv, image_send, image_recv,
):
    views, columns = sino_ref.shape
    groups = SIDE * SIDE
    chunks = columns // LANES
    per_block = chunks // BLOCKS
    slices = lax.axis_size("cuts")
    group = lax.axis_index("angle")
    cut = lax.axis_index("cuts")

    mine = [group == y * SIDE + z for y, z in OWNERS]
    is_owner = functools.reduce(jnp.logical_or, mine)
    block_id = sum(jnp.where(hit, b, 0) for b, hit in enumerate(mine))
    owner_int = is_owner.astype(jnp.int32)
    has_side = [cut > 0, True, cut < slices - 1]

    def rows(index):
        return pl.ds(2 * index, 2)

    barrier = pltpu.get_barrier_semaphore()
    sino_copy = pltpu.make_async_copy(sino_any, sino_ref, local_sem.at[0])
    sino_copy.start()

    @pl.when(is_owner)
    def _():
        bank_copy = pltpu.make_async_copy(bank_any, bank_ref, local_sem.at[1])
        index_copy = pltpu.make_async_copy(index_any, index_ref, local_sem.at[2])
        taps_copy = pltpu.make_async_copy(taps_any, taps_ref, local_sem.at[3])
        bank_copy.start()
        index_copy.start()
        taps_copy.start()

        def announce(step, carry):
            for side in range(3):
                target = lax.rem(cut + side - 1 + slices, slices)
                valid = step != group if side == 1 else has_side[side]

                @pl.when(valid)
                def _():
                    pl.semaphore_signal(barrier, inc=1, device_id=(step, target), device_id_type=MESH)

            return carry

        lax.fori_loop(0, groups, announce, 0)
        bank_copy.wait()
        index_copy.wait()
        taps_copy.wait()

    sino_copy.wait()
    total = jnp.sum(sino_ref[...].astype(jnp.float32), axis=0, keepdims=True)
    sub = lax.broadcasted_iota(jnp.int32, (8, LANES), 0)
    tiles = []
    for t in range(chunks // 8):
        tile = jnp.zeros((8, LANES), jnp.float32)
        for i in range(8):
            c = t * 8 + i
            piece = jnp.broadcast_to(total[:, c * LANES : (c + 1) * LANES], (8, LANES))
            tile = jnp.where(sub == i, piece, tile)
        tiles.append(tile)
    summed = jnp.concatenate(tiles, axis=0)
    lane = lax.broadcasted_iota(jnp.int32, (chunks, LANES), 1)
    chunk = lax.broadcasted_iota(jnp.int32, (chunks, LANES), 0)
    shift = lax.div(group, 2) - groups // 4
    for r, amount in enumerate((-1 - shift, shift)):
        turned = pltpu.roll(summed, lax.rem(amount + LANES, LANES), 1)
        before = jnp.where(chunk == 0, 0.0, pltpu.roll(turned, 1, 0))
        after = jnp.where(chunk == chunks - 1, 0.0, pltpu.roll(turned, chunks - 1, 0))
        source = lane - amount
        leaf = jnp.where(source < 0, before, jnp.where(source >= LANES, after, turned))
        for b in range(BLOCKS):
            send_buf[2 * b + r, :, :] = leaf[b * per_block : (b + 1) * per_block, :]

    n_sides = 1 + (cut > 0).astype(jnp.int32) + (cut < slices - 1).astype(jnp.int32)
    pl.semaphore_wait(barrier, n_sides * BLOCKS - owner_int)

    def leaf_copy(b, side):
        y, z = OWNERS[b]
        return pltpu.make_async_remote_copy(
            src_ref=send_buf.at[rows(b)],
            dst_ref=leaf_buf.at[2 - side, rows(group)],
            send_sem=leaf_send,
            recv_sem=leaf_recv.at[2 - side],
            device_id=(y * SIDE + z, lax.rem(cut + side - 1 + slices, slices)),
            device_id_type=MESH,
        )

    for b in range(BLOCKS):
        for side in range(3):
            if side == 1:
                valid = jnp.logical_not(mine[b])
            else:
                valid = has_side[side]

            @pl.when(valid)
            def _():
                leaf_copy(b, side).start()

    @pl.when(is_owner)
    def _():
        leaf_buf[1, rows(group)] = send_buf[rows(block_id)]
        tree = tree_matrix(bank_ref, index_ref, 6, 2 * groups) * (1.0 / math.sqrt(views))
        high, low = parts_of(tree)
        tree_buf[...] = jnp.concatenate([high, low, high], axis=1)
        for side in range(3):
            count = groups - 1 if side == 1 else groups

            @pl.when(has_side[side])
            def _():
                done = leaf_buf.at[side, pl.ds(0, 2 * count)]
                pltpu.make_async_copy(done, done, leaf_recv.at[side]).wait()

        mixed = []
        for i in range(per_block):
            term = None
            for side in range(3):
                value = taps_ref[side] * leaf_buf[side, :, i, :]
                if side != 1:
                    value = jnp.where(has_side[side], value, 0.0)
                term = value if term is None else term + value
            mixed.append(term)
        high, low = parts_of(jnp.concatenate(mixed, axis=1))
        image = jnp.dot(
            tree_buf[...], jnp.concatenate([high, high, low], axis=0), preferred_element_type=jnp.float32
        )
        for i in range(per_block):
            result_buf[:, i, :] = image[:, i * LANES : (i + 1) * LANES]

        image_buf[rows(block_id)] = result_buf[rows(group)]

        def give(step, carry):
            @pl.when(step != group)
            def _():
                pltpu.make_async_remote_copy(
                    src_ref=result_buf.at[rows(step)],
                    dst_ref=image_buf.at[rows(block_id)],
                    send_sem=image_send,
                    recv_sem=image_recv,
                    device_id=(step, cut),
                    device_id_type=MESH,
                ).start()

            return carry

        lax.fori_loop(0, groups, give, 0)
        got = image_buf.at[pl.ds(0, 2 * (BLOCKS - 1))]
        pltpu.make_async_copy(got, got, image_recv).wait()

    @pl.when(jnp.logical_not(is_owner))
    def _():
        pltpu.make_async_copy(image_buf, image_buf, image_recv).wait()

    for b in range(BLOCKS):
        for i in range(per_block):
            c = b * per_block + i
            out_ref[:, c * LANES : (c + 1) * LANES] = image_buf[2 * b : 2 * b + 2, i, :]

    for b in range(BLOCKS):
        for side in range(3):
            if side == 1:
                valid = jnp.logical_not(mine[b])
            else:
                valid = has_side[side]

            @pl.when(valid)
            def _():
                leaf_copy(b, side).wait_send()

    @pl.when(is_owner)
    def _():
        sent = result_buf.at[pl.ds(0, 2 * (groups - 1))]
        pltpu.make_async_copy(sent, sent, image_send).wait()


def shards(sinogram, estimate, interp_bank, interp_index, slice_taps):
    _, views, columns = sinogram.shape
    groups = SIDE * SIDE
    chunks = columns // LANES
    per_block = chunks // BLOCKS
    size = 2 * groups
    bank = jnp.swapaxes(interp_bank, 1, 2)
    operands = (sinogram[0], bank, interp_index.reshape(1, -1), slice_taps)
    held = [pltpu.with_memory_space_constraint(x, pltpu.HBM) for x in operands]
    mixed = pl.pallas_call(
        kernel,
        out_shape=pltpu.VMEM((2, columns), jnp.float32),
        in_specs=[
            pl.BlockSpec(memory_space=pltpu.HBM),
            pl.BlockSpec(memory_space=pltpu.HBM),
            pl.BlockSpec(memory_space=pltpu.HBM),
            pl.BlockSpec(memory_space=pltpu.HBM),
        ],
        out_specs=pl.BlockSpec(memory_space=pltpu.VMEM),
        scratch_shapes=[
            pltpu.VMEM((views, columns), jnp.bfloat16),
            pltpu.VMEM(bank.shape, jnp.float32),
            pltpu.VMEM((1, size), jnp.int32),
            pltpu.SMEM((3,), jnp.float32),
            pltpu.VMEM((2 * BLOCKS, per_block, LANES), jnp.float32),
            pltpu.VMEM((3, size, per_block, LANES), jnp.float32),
            pltpu.VMEM((size, per_block, LANES), jnp.float32),
            pltpu.VMEM((2 * BLOCKS, per_block, LANES), jnp.float32),
            pltpu.VMEM((size, 3 * size), jnp.bfloat16),
            pltpu.SemaphoreType.DMA((4,)),
            pltpu.SemaphoreType.DMA,
            pltpu.SemaphoreType.DMA((3,)),
            pltpu.SemaphoreType.DMA,
            pltpu.SemaphoreType.DMA,
        ],
        compiler_params=pltpu.CompilerParams(
            collective_id=0, has_side_effects=True, vmem_limit_bytes=32 * 1024 * 1024
        ),
    )(*held)
    return (estimate[0].astype(jnp.float32) - mixed)[None]


def solution(mesh):
    in_specs = (P("cuts", "angle", None), P("cuts", "angle", None), P(), P(), P())
    out_specs = P("cuts", "angle", None)
    return jax.shard_map(shards, mesh=mesh, in_specs=in_specs, out_specs=out_specs, check_vma=False)
```

```python
import functools
import math

import jax
import jax.numpy as jnp
from jax import lax
from jax.experimental import pallas as pl
from jax.experimental.pallas import tpu as pltpu
from jax.sharding import PartitionSpec as P

MESH = pl.DeviceIdType.MESH
SIDE = 8
CORES = 2
LANES = 128
GROUPS = SIDE * SIDE
SIZE = 2 * GROUPS
OWNERS = ((0, 1), (1, 0), (2, 0), (3, 0), (4, 0), (5, 0), (6, 0), (7, 0))
BLOCKS = len(OWNERS) * CORES


def parts_of(value):
    high = value.astype(jnp.bfloat16)
    low = (value - high.astype(jnp.float32)).astype(jnp.bfloat16)
    return high, low


def iota(shape, dim):
    return lax.broadcasted_iota(jnp.int32, shape, dim)


def tree_matrix(bank_ref, index_ref):
    kinds, half = bank_ref.shape[:2]
    levels = GROUPS.bit_length() - 1
    index = jnp.broadcast_to(index_ref[...].astype(jnp.float32), (8, SIZE))
    product = None
    for level in range(1, levels + 1):
        width = SIZE >> level
        row, col = iota((SIZE, SIZE), 0), iota((SIZE, SIZE), 1)
        chosen = (row == (1 << level) + col // width).astype(jnp.float32)
        kind = jnp.dot(index, chosen, preferred_element_type=jnp.float32)[0:1]
        block = jnp.zeros((2 * width, SIZE), jnp.float32)
        pick = iota((half, SIZE), 0) == iota((half, SIZE), 1) % width
        for k in range(kinds):
            place = jnp.where(pick & (jnp.abs(kind - k) < 0.5), 1.0, 0.0)
            block += lax.dot_general(
                bank_ref[k, :, :],
                place,
                (((0,), (0,)), ((), ())),
                precision=lax.Precision.HIGHEST,
                preferred_element_type=jnp.float32,
            )[: 2 * width]
        if 2 * width < 8:
            block = jnp.concatenate([block] * (8 // (2 * width)), axis=0)
        factor = jnp.concatenate([block] * (SIZE // block.shape[0]), axis=0)
        factor = jnp.where(row // (2 * width) == col // (2 * width), factor, 0.0)
        if product is None:
            product = factor
        else:
            product = jnp.dot(
                product, factor, precision=lax.Precision.HIGHEST, preferred_element_type=jnp.float32
            )
    return product


def far_first(turn):
    back = lax.rem(turn, 2)
    return SIDE // 2 + (1 - 2 * back) * lax.div(turn + back, 2)


def slot_of(group):
    return lax.rem(group, 2) * (GROUPS // 2) + lax.div(group, 2)


def kernel(
    sino_any, bank_any, index_any, taps_any, out_ref,
    sino_ref, bank_ref, index_ref, taps_ref, send_buf, leaf_buf, result_buf, image_buf, tree_buf,
    local_sem, leaf_send, leaf_recv, image_send, image_recv,
):
    views, columns = sino_ref.shape
    per_block = columns // LANES // BLOCKS
    window = per_block + 1
    slices = lax.axis_size("cuts")
    group = lax.axis_index("angle")
    cut = lax.axis_index("cuts")
    core = lax.rem(cut, CORES)
    first = cut - core
    here = [group == y * SIDE + z for y, z in OWNERS]
    is_owner = functools.reduce(jnp.logical_or, here)
    mine = core + sum(jnp.where(hit, CORES * i, 0) for i, hit in enumerate(here))
    half = GROUPS // 2

    has_side = [first > 0, True, True, first + CORES < slices]
    side_cut = [lax.rem(first + side - 1 + slices, slices) for side in range(4)]

    barrier = pltpu.get_barrier_semaphore()
    sino_copy = pltpu.make_async_copy(sino_any, sino_ref, local_sem.at[0])
    sino_copy.start()

    @pl.when(is_owner)
    def _():
        bank_copy = pltpu.make_async_copy(bank_any, bank_ref, local_sem.at[1])
        index_copy = pltpu.make_async_copy(index_any, index_ref, local_sem.at[2])
        taps_copy = pltpu.make_async_copy(taps_any, taps_ref, local_sem.at[3])
        bank_copy.start()
        index_copy.start()
        taps_copy.start()

        def announce(step, carry):
            y = lax.rem(lax.div(group, SIDE) + far_first(lax.rem(step, SIDE)), SIDE)
            z = lax.rem(group + far_first(lax.div(step, SIDE)), SIDE)
            target = y * SIDE + z
            for side in range(4):
                valid = has_side[side]
                if side in (1, 2):
                    valid = jnp.logical_or(target != group, core != side - 1)

                @pl.when(valid)
                def _():
                    pl.semaphore_signal(barrier, inc=1, device_id=(target, side_cut[side]), device_id_type=MESH)

            return carry

        lax.fori_loop(0, GROUPS, announce, 0)
        bank_copy.wait()
        index_copy.wait()
        taps_copy.wait()

    sino_copy.wait()
    total = jnp.sum(sino_ref[...].astype(jnp.float32), axis=0, keepdims=True)
    margin = jnp.zeros((1, LANES // 2), jnp.float32)
    total = jnp.concatenate([margin, total, margin], axis=1)
    for b in range(BLOCKS):
        for c in range(window):
            start = (b * per_block + c) * LANES
            send_buf[b, c : c + 1, :] = total[:, start : start + LANES]

    other = jnp.where(core == 0, cut - 1, cut + 1)
    has_other = jnp.where(core == 0, cut > 0, cut < slices - 1)
    other_first = lax.rem(jnp.where(core == 0, cut - CORES, cut + 1) + slices, slices)
    other_side = jnp.where(core == 0, 3, 0)
    n_owners = BLOCKS + jnp.where(has_other, BLOCKS, 0) - jnp.where(is_owner, 1, 0)
    pl.semaphore_wait(barrier, n_owners)

    def leaf_copy(b, plane):
        base, side = (first, 1 + core) if plane == 0 else (other_first, other_side)
        return pltpu.make_async_remote_copy(
            src_ref=send_buf.at[b],
            dst_ref=leaf_buf.at[side, slot_of(group)],
            send_sem=leaf_send,
            recv_sem=leaf_recv.at[side],
            device_id=(OWNERS[b // CORES][0] * SIDE + OWNERS[b // CORES][1], base + b % CORES),
            device_id_type=MESH,
        )

    def each_leaf(act):
        for plane in range(2):
            for b in range(BLOCKS):
                valid = has_other
                if plane == 0:
                    valid = jnp.logical_not(jnp.logical_and(is_owner, mine == b))

                @pl.when(valid)
                def _():
                    act(leaf_copy(b, plane))

    each_leaf(lambda copy: copy.start())

    @pl.when(is_owner)
    def _():
        leaf_buf[1 + core, slot_of(group)] = send_buf[mine]
        row, col = iota((SIZE, SIZE), 0), iota((SIZE, SIZE), 1)
        natural = 4 * (col % half) + 2 * (col % GROUPS // half) + col // GROUPS
        order = (row == natural).astype(jnp.bfloat16)
        tree = tree_matrix(bank_ref, index_ref) * (1.0 / math.sqrt(views))
        high, low = [
            jnp.dot(part, order, preferred_element_type=jnp.float32).astype(jnp.bfloat16) for part in parts_of(tree)
        ]
        tree_buf[...] = jnp.concatenate([high, low, high], axis=1)

        for side in range(4):
            def wait(count):
                done = leaf_buf.at[side, pl.ds(0, count)]
                pltpu.make_async_copy(done, done, leaf_recv.at[side]).wait()

            if side in (1, 2):
                own = core == side - 1
                pl.when(own)(lambda: wait(GROUPS - 1))
                pl.when(jnp.logical_not(own))(lambda: wait(GROUPS))
            else:
                pl.when(has_side[side])(lambda: wait(GROUPS))

        lane, place = iota((half, LANES), 1), iota((half, LANES), 0)
        moved = [half // 2 - 1 - place, place - half // 2]
        back = lax.rem(lane - moved[0] + LANES // 2 + LANES, LANES)
        leaves = []
        for e in range(CORES):
            mixed = [[None] * 2 for _ in range(window)]
            for c in range(window):
                term = None
                for tap in range(3):
                    value = taps_ref[tap] * leaf_buf[e + tap, :, c, :]
                    if e + tap in (0, 3):
                        value = jnp.where(has_side[e + tap], value, 0.0)
                    term = value if term is None else term + value
                mixed[c] = [term[:half], term[half:]]
            rows = []
            for r in range(2):
                for h in range(2):
                    turned = []
                    for c in range(window):
                        if r == 1:
                            turned.append(
                                pltpu.roll(mixed[c][h], LANES // 2 - half // 2, 1, stride=1, stride_axis=0)
                            )
                        else:
                            turned.append(jnp.take_along_axis(mixed[c][h], back, axis=1))
                    rows.append(
                        jnp.concatenate(
                            [
                                jnp.where(lane - moved[r] < LANES // 2, turned[i], turned[i + 1])
                                for i in range(per_block)
                            ],
                            axis=1,
                        )
                    )
            leaves.append(jnp.concatenate(rows, axis=0))
        high, low = parts_of(jnp.concatenate(leaves, axis=1))
        image = jnp.dot(
            tree_buf[...], jnp.concatenate([high, high, low], axis=0), preferred_element_type=jnp.float32
        )
        for e in range(CORES):
            for i in range(per_block):
                start = (e * per_block + i) * LANES
                result_buf[e, :, i, :] = image[:, start : start + LANES]

        image_buf[pl.ds(2 * mine, 2)] = result_buf[core, pl.ds(2 * group, 2)]

        def give(step, carry):
            turn = lax.rem(step, SIDE)
            y = jnp.where(turn < SIDE // 2, turn, SIDE + SIDE // 2 - 1 - turn)
            target = y * SIDE + lax.div(step, SIDE)
            for e in range(CORES):

                @pl.when(jnp.logical_or(target != group, core != e))
                def _():
                    pltpu.make_async_remote_copy(
                        src_ref=result_buf.at[e, pl.ds(2 * target, 2)],
                        dst_ref=image_buf.at[pl.ds(2 * mine, 2)],
                        send_sem=image_send,
                        recv_sem=image_recv,
                        device_id=(target, first + e),
                        device_id_type=MESH,
                    ).start()

            return carry

        lax.fori_loop(0, GROUPS, give, 0)
        got = image_buf.at[pl.ds(0, 2 * (BLOCKS - 1))]
        pltpu.make_async_copy(got, got, image_recv).wait()

    @pl.when(jnp.logical_not(is_owner))
    def _():
        pltpu.make_async_copy(image_buf, image_buf, image_recv).wait()

    for b in range(BLOCKS):
        for i in range(per_block):
            c = b * per_block + i
            out_ref[:, c * LANES : (c + 1) * LANES] = image_buf[2 * b : 2 * b + 2, i, :]

    each_leaf(lambda copy: copy.wait_send())

    @pl.when(is_owner)
    def _():
        for e in range(CORES):
            own = core == e

            def wait(count):
                sent = result_buf.at[e, pl.ds(0, 2 * count)]
                pltpu.make_async_copy(sent, sent, image_send).wait()

            pl.when(own)(lambda: wait(GROUPS - 1))
            pl.when(jnp.logical_not(own))(lambda: wait(GROUPS))


def shards(sinogram, estimate, interp_bank, interp_index, slice_taps):
    _, views, columns = sinogram.shape
    per_block = columns // LANES // BLOCKS
    bank = jnp.swapaxes(interp_bank, 1, 2)
    operands = (sinogram[0], bank, interp_index.reshape(1, -1), slice_taps)
    held = [pltpu.with_memory_space_constraint(x, pltpu.HBM) for x in operands]
    mixed = pl.pallas_call(
        kernel,
        out_shape=pltpu.VMEM((2, columns), jnp.float32),
        in_specs=[pl.BlockSpec(memory_space=pltpu.HBM)] * 4,
        out_specs=pl.BlockSpec(memory_space=pltpu.VMEM),
        scratch_shapes=[
            pltpu.VMEM((views, columns), jnp.bfloat16),
            pltpu.VMEM(bank.shape, jnp.float32),
            pltpu.VMEM((1, SIZE), jnp.int32),
            pltpu.SMEM((3,), jnp.float32),
            pltpu.VMEM((BLOCKS, per_block + 1, LANES), jnp.float32),
            pltpu.VMEM((4, GROUPS, per_block + 1, LANES), jnp.float32),
            pltpu.VMEM((CORES, SIZE, per_block, LANES), jnp.float32),
            pltpu.VMEM((2 * BLOCKS, per_block, LANES), jnp.float32),
            pltpu.VMEM((SIZE, 3 * SIZE), jnp.bfloat16),
            pltpu.SemaphoreType.DMA((4,)),
            pltpu.SemaphoreType.DMA,
            pltpu.SemaphoreType.DMA((4,)),
            pltpu.SemaphoreType.DMA,
            pltpu.SemaphoreType.DMA,
        ],
        compiler_params=pltpu.CompilerParams(
            collective_id=0, has_side_effects=True, vmem_limit_bytes=32 * 1024 * 1024
        ),
    )(*held)
    return (estimate[0].astype(jnp.float32) - mixed)[None]


def solution(mesh):
    in_specs = (P("cuts", "angle", None), P("cuts", "angle", None), P(), P(), P())
    out_specs = P("cuts", "angle", None)
    return jax.shard_map(shards, mesh=mesh, in_specs=in_specs, out_specs=out_specs, check_vma=False)
```

```python
import functools
import math

import jax
import jax.numpy as jnp
from jax import lax
from jax.experimental import pallas as pl
from jax.experimental.pallas import tpu as pltpu
from jax.sharding import PartitionSpec as P

MESH = pl.DeviceIdType.MESH
SIDE = 8
CORES = 2
LANES = 128
GROUPS = SIDE * SIDE
SIZE = 2 * GROUPS
OWNERS = ((0, 1), (1, 0), (2, 0), (3, 0), (0, 2), (5, 0), (6, 0), (7, 0))
BLOCKS = len(OWNERS) * CORES
QUARTER = SIDE // 4
HALF = GROUPS // 2


def parts_of(value):
    high = value.astype(jnp.bfloat16)
    low = (value - high.astype(jnp.float32)).astype(jnp.bfloat16)
    return high, low


def iota(shape, dim):
    return lax.broadcasted_iota(jnp.int32, shape, dim)


def tree_matrix(bank_ref, index_ref):
    kinds, half = bank_ref.shape[:2]
    levels = GROUPS.bit_length() - 1
    index = jnp.broadcast_to(index_ref[...].astype(jnp.float32), (8, SIZE))
    product = None
    for level in range(1, levels + 1):
        width = SIZE >> level
        row, col = iota((SIZE, SIZE), 0), iota((SIZE, SIZE), 1)
        chosen = (row == (1 << level) + col // width).astype(jnp.float32)
        kind = jnp.dot(index, chosen, preferred_element_type=jnp.float32)[0:1]
        block = jnp.zeros((2 * width, SIZE), jnp.float32)
        pick = iota((half, SIZE), 0) == iota((half, SIZE), 1) % width
        for k in range(kinds):
            place = jnp.where(pick & (jnp.abs(kind - k) < 0.5), 1.0, 0.0)
            block += lax.dot_general(
                bank_ref[k, :, :],
                place,
                (((0,), (0,)), ((), ())),
                precision=lax.Precision.HIGHEST,
                preferred_element_type=jnp.float32,
            )[: 2 * width]
        if 2 * width < 8:
            block = jnp.concatenate([block] * (8 // (2 * width)), axis=0)
        factor = jnp.concatenate([block] * (SIZE // block.shape[0]), axis=0)
        factor = jnp.where(row // (2 * width) == col // (2 * width), factor, 0.0)
        if product is None:
            product = factor
        else:
            product = jnp.dot(
                product, factor, precision=lax.Precision.HIGHEST, preferred_element_type=jnp.float32
            )
    return product


def far_first(turn):
    back = lax.rem(turn, 2)
    return SIDE // 2 + (1 - 2 * back) * lax.div(turn + back, 2)


def slot_of(group):
    y, z = lax.div(group, SIDE), lax.rem(group, SIDE)
    late, rest = lax.div(z, SIDE // 2), lax.rem(z, SIDE // 2)
    return ((late * 2 + lax.rem(rest, 2)) * QUARTER + lax.div(rest, 2)) * SIDE + y


def kernel(
    sino_any, bank_any, index_any, taps_any, out_ref,
    sino_ref, bank_ref, index_ref, taps_ref, send_buf, leaf_buf, result_buf, image_buf, tree_buf, early_buf,
    local_sem, leaf_send, leaf_recv, image_send, image_recv,
):
    views, columns = sino_ref.shape
    per_block = columns // LANES // BLOCKS
    window = per_block + 1
    slices = lax.axis_size("cuts")
    group = lax.axis_index("angle")
    cut = lax.axis_index("cuts")
    core = lax.rem(cut, CORES)
    first = cut - core
    here = [group == y * SIDE + z for y, z in OWNERS]
    is_owner = functools.reduce(jnp.logical_or, here)
    mine = core + sum(jnp.where(hit, CORES * i, 0) for i, hit in enumerate(here))
    late = lax.div(lax.rem(group, SIDE), SIDE // 2)

    has_side = [first > 0, True, True, first + CORES < slices]
    side_cut = [lax.rem(first + side - 1 + slices, slices) for side in range(4)]

    barrier = pltpu.get_barrier_semaphore()
    parts = [pl.ds(p * (columns // 2), columns // 2) for p in range(2)]
    sino_copies = [
        pltpu.make_async_copy(sino_any.at[:, part], sino_ref.at[:, part], local_sem.at[p])
        for p, part in enumerate(parts)
    ]
    for copy in sino_copies:
        copy.start()

    @pl.when(is_owner)
    def _():
        bank_copy = pltpu.make_async_copy(bank_any, bank_ref, local_sem.at[2])
        index_copy = pltpu.make_async_copy(index_any, index_ref, local_sem.at[3])
        taps_copy = pltpu.make_async_copy(taps_any, taps_ref, local_sem.at[4])
        bank_copy.start()
        index_copy.start()
        taps_copy.start()

        def announce(step, carry):
            y = lax.rem(lax.div(group, SIDE) + far_first(lax.rem(step, SIDE)), SIDE)
            z = lax.rem(group + far_first(lax.div(step, SIDE)), SIDE)
            target = y * SIDE + z
            for side in range(4):
                valid = has_side[side]
                if side in (1, 2):
                    valid = jnp.logical_or(target != group, core != side - 1)

                @pl.when(valid)
                def _():
                    pl.semaphore_signal(barrier, inc=1, device_id=(target, side_cut[side]), device_id_type=MESH)

            return carry

        lax.fori_loop(0, GROUPS, announce, 0)
        bank_copy.wait()
        index_copy.wait()
        taps_copy.wait()

    margin = jnp.zeros((1, LANES // 2), jnp.float32)
    pending = margin
    row = 0
    for part, copy in zip(parts, sino_copies):
        copy.wait()
        total = jnp.sum(sino_ref[:, part].astype(jnp.float32), axis=0, keepdims=True)
        if part is parts[-1]:
            total = jnp.concatenate([total, margin], axis=1)
        total = jnp.concatenate([pending, total], axis=1)
        for c in range(total.shape[1] // LANES):
            for b in range(BLOCKS):
                if 0 <= row - b * per_block < window:
                    send_buf[b, row - b * per_block : row - b * per_block + 1, :] = total[:, c * LANES : (c + 1) * LANES]
            row += 1
        pending = total[:, total.shape[1] // LANES * LANES :]

    has_other = jnp.where(core == 0, cut > 0, cut < slices - 1)
    other_first = lax.rem(jnp.where(core == 0, cut - CORES, cut + 1) + slices, slices)
    other_side = jnp.where(core == 0, 3, 0)
    n_owners = BLOCKS + jnp.where(has_other, BLOCKS, 0) - jnp.where(is_owner, 1, 0)
    pl.semaphore_wait(barrier, n_owners)

    def leaf_copy(b, turn):
        own = core != turn
        side = jnp.where(own, 1 + core, other_side)
        y, z = OWNERS[b // CORES]
        return pltpu.make_async_remote_copy(
            src_ref=send_buf.at[b],
            dst_ref=leaf_buf.at[side, slot_of(group)],
            send_sem=leaf_send,
            recv_sem=leaf_recv.at[side, late],
            device_id=(y * SIDE + z, jnp.where(own, first, other_first) + b % CORES),
            device_id_type=MESH,
        )

    for turn in range(2):
        valid = jnp.where(core != turn, True, has_other)

        @pl.when(jnp.logical_and(valid, jnp.logical_not(is_owner)))
        def _():
            for b in range(BLOCKS):
                leaf_copy(b, turn).start()

        @pl.when(jnp.logical_and(valid, is_owner))
        def _():
            for b in range(BLOCKS):

                @pl.when(jnp.logical_or(core == turn, mine != b))
                def _():
                    leaf_copy(b, turn).start()

    def all_left(count):
        sent = send_buf.at[pl.ds(0, count)]
        pltpu.make_async_copy(sent, sent, leaf_send).wait()

    pl.when(is_owner)(lambda: all_left(BLOCKS - 1))
    pl.when(jnp.logical_not(is_owner))(lambda: all_left(BLOCKS))
    pl.when(has_other)(lambda: all_left(BLOCKS))

    @pl.when(is_owner)
    def _():
        leaf_buf[1 + core, slot_of(group)] = send_buf[mine]
        row, col = iota((SIZE, SIZE), 0), iota((SIZE, SIZE), 1)
        place = lax.rem(col, HALF)
        z = (
            col // GROUPS * (SIDE // 2)
            + lax.rem(place // SIDE, QUARTER) * 2
            + place // (SIDE * QUARTER)
        )
        natural = 2 * (lax.rem(place, SIDE) * SIDE + z) + lax.rem(col // HALF, 2)
        order = (row == natural).astype(jnp.bfloat16)
        tree = tree_matrix(bank_ref, index_ref) * (1.0 / math.sqrt(views))
        high, low = [
            jnp.dot(part, order, preferred_element_type=jnp.float32).astype(jnp.bfloat16) for part in parts_of(tree)
        ]
        for part in range(2):
            span = slice(part * GROUPS, (part + 1) * GROUPS)
            tree_buf[part] = jnp.concatenate([high[:, span], low[:, span], high[:, span]], axis=1)

        lane, place = iota((HALF, LANES), 1), iota((HALF, LANES), 0)
        image = None
        for part in range(2):
            for side in range(4):
                def wait(count):
                    done = leaf_buf.at[side, pl.ds(0, count)]
                    pltpu.make_async_copy(done, done, leaf_recv.at[side, part]).wait()

                if side in (1, 2) and part == 0:
                    own = core == side - 1
                    pl.when(own)(lambda: wait(HALF - 1))
                    pl.when(jnp.logical_not(own))(lambda: wait(HALF))
                else:
                    pl.when(has_side[side])(lambda: wait(HALF))

            pair = lax.rem(place, SIDE) * (SIDE // 2) + lax.rem(place // SIDE, QUARTER) + part * QUARTER
            moved = [GROUPS // 4 - 1 - pair, pair - GROUPS // 4]
            back = lax.rem(lane - moved[0] + LANES // 2 + LANES, LANES)
            leaves = []
            for e in range(CORES):
                mixed = []
                for c in range(window):
                    term = None
                    for tap in range(3):
                        value = taps_ref[tap] * leaf_buf[e + tap, part * HALF : (part + 1) * HALF, c, :]
                        if e + tap in (0, 3):
                            value = jnp.where(has_side[e + tap], value, 0.0)
                        term = value if term is None else term + value
                    mixed.append(term)
                rows = []
                for r in range(2):
                    turned = []
                    for c in range(window):
                        if r == 0:
                            turned.append(jnp.take_along_axis(mixed[c], back, axis=1))
                            continue
                        pieces = []
                        for k in range(HALF // SIDE):
                            base = LANES // 2 - GROUPS // 4 + part * QUARTER + k % QUARTER
                            piece = mixed[c][k * SIDE : (k + 1) * SIDE]
                            pieces.append(pltpu.roll(piece, base, 1, stride=SIDE // 2, stride_axis=0))
                        turned.append(jnp.concatenate(pieces, axis=0))
                    rows.append(
                        jnp.concatenate(
                            [
                                jnp.where(lane - moved[r] < LANES // 2, turned[i], turned[i + 1])
                                for i in range(per_block)
                            ],
                            axis=1,
                        )
                    )
                leaves.append(jnp.concatenate(rows, axis=0))
            high, low = parts_of(jnp.concatenate(leaves, axis=1))
            product = jnp.dot(
                tree_buf[part], jnp.concatenate([high, high, low], axis=0), preferred_element_type=jnp.float32
            )
            if part == 0:
                early_buf[...] = product
            else:
                image = early_buf[...] + product
        for e in range(CORES):
            for i in range(per_block):
                start = (e * per_block + i) * LANES
                result_buf[e, :, i, :] = image[:, start : start + LANES]

        image_buf[pl.ds(2 * mine, 2)] = result_buf[core, pl.ds(2 * group, 2)]

        def give(step, carry):
            turn = lax.rem(step, SIDE)
            y = jnp.where(turn < SIDE // 2, turn, SIDE + SIDE // 2 - 1 - turn)
            target = y * SIDE + lax.div(step, SIDE)
            for e in range(CORES):

                @pl.when(jnp.logical_or(target != group, core != e))
                def _():
                    pltpu.make_async_remote_copy(
                        src_ref=result_buf.at[e, pl.ds(2 * target, 2)],
                        dst_ref=image_buf.at[pl.ds(2 * mine, 2)],
                        send_sem=image_send,
                        recv_sem=image_recv,
                        device_id=(target, first + e),
                        device_id_type=MESH,
                    ).start()

            return carry

        lax.fori_loop(0, GROUPS, give, 0)
        got = image_buf.at[pl.ds(0, 2 * (BLOCKS - 1))]
        pltpu.make_async_copy(got, got, image_recv).wait()

    @pl.when(jnp.logical_not(is_owner))
    def _():
        pltpu.make_async_copy(image_buf, image_buf, image_recv).wait()

    for b in range(BLOCKS):
        for i in range(per_block):
            c = b * per_block + i
            out_ref[:, c * LANES : (c + 1) * LANES] = image_buf[2 * b : 2 * b + 2, i, :]

    @pl.when(is_owner)
    def _():
        for e in range(CORES):
            own = core == e

            def wait(count):
                sent = result_buf.at[e, pl.ds(0, 2 * count)]
                pltpu.make_async_copy(sent, sent, image_send).wait()

            pl.when(own)(lambda: wait(GROUPS - 1))
            pl.when(jnp.logical_not(own))(lambda: wait(GROUPS))


def shards(sinogram, estimate, interp_bank, interp_index, slice_taps):
    _, views, columns = sinogram.shape
    per_block = columns // LANES // BLOCKS
    bank = jnp.swapaxes(interp_bank, 1, 2)
    operands = (sinogram[0], bank, interp_index.reshape(1, -1), slice_taps)
    held = [pltpu.with_memory_space_constraint(x, pltpu.HBM) for x in operands]
    mixed = pl.pallas_call(
        kernel,
        out_shape=pltpu.VMEM((2, columns), jnp.float32),
        in_specs=[pl.BlockSpec(memory_space=pltpu.HBM)] * 4,
        out_specs=pl.BlockSpec(memory_space=pltpu.VMEM),
        scratch_shapes=[
            pltpu.VMEM((views, columns), jnp.bfloat16),
            pltpu.VMEM(bank.shape, jnp.float32),
            pltpu.VMEM((1, SIZE), jnp.int32),
            pltpu.SMEM((3,), jnp.float32),
            pltpu.VMEM((BLOCKS, per_block + 1, LANES), jnp.float32),
            pltpu.VMEM((4, GROUPS, per_block + 1, LANES), jnp.float32),
            pltpu.VMEM((CORES, SIZE, per_block, LANES), jnp.float32),
            pltpu.VMEM((2 * BLOCKS, per_block, LANES), jnp.float32),
            pltpu.VMEM((2, SIZE, 3 * GROUPS), jnp.bfloat16),
            pltpu.VMEM((SIZE, CORES * columns // BLOCKS), jnp.float32),
            pltpu.SemaphoreType.DMA((5,)),
            pltpu.SemaphoreType.DMA,
            pltpu.SemaphoreType.DMA((4, 2)),
            pltpu.SemaphoreType.DMA,
            pltpu.SemaphoreType.DMA,
        ],
        compiler_params=pltpu.CompilerParams(
            collective_id=0, has_side_effects=True, vmem_limit_bytes=32 * 1024 * 1024
        ),
    )(*held)
    return (estimate[0].astype(jnp.float32) - mixed)[None]


def solution(mesh):
    in_specs = (P("cuts", "angle", None), P("cuts", "angle", None), P(), P(), P())
    out_specs = P("cuts", "angle", None)
    return jax.shard_map(shards, mesh=mesh, in_specs=in_specs, out_specs=out_specs, check_vma=False)
```

```python
import functools
import math

import jax
import jax.numpy as jnp
from jax import lax
from jax.experimental import pallas as pl
from jax.experimental.pallas import tpu as pltpu
from jax.sharding import PartitionSpec as P

MESH = pl.DeviceIdType.MESH
SIDE = 8
CORES = 2
LANES = 128
GROUPS = SIDE * SIDE
SIZE = 2 * GROUPS
OWNERS = ((1, 0, 0), (1, 1, 1), (1, 1, 0), (2, 0, 0), (2, 0, 1), (7, 0, 0), (7, 0, 1), (6, 0, 0), (6, 0, 1), (3, 0, 0), (3, 0, 1), (5, 0, 0), (5, 0, 1), (0, 1, 0), (0, 1, 1), (4, 0, 0))
BLOCKS = len(OWNERS)
QUARTER = SIDE // 4
HALF = GROUPS // 2


def parts_of(value):
    high = value.astype(jnp.bfloat16)
    low = (value - high.astype(jnp.float32)).astype(jnp.bfloat16)
    return high, low


def iota(shape, dim):
    return lax.broadcasted_iota(jnp.int32, shape, dim)


def tree_matrix(bank_ref, index_ref):
    kinds, half = bank_ref.shape[:2]
    levels = GROUPS.bit_length() - 1
    index = jnp.broadcast_to(index_ref[...].astype(jnp.float32), (8, SIZE))
    product = None
    for level in range(1, levels + 1):
        width = SIZE >> level
        row, col = iota((SIZE, SIZE), 0), iota((SIZE, SIZE), 1)
        chosen = (row == (1 << level) + col // width).astype(jnp.float32)
        kind = jnp.dot(index, chosen, preferred_element_type=jnp.float32)[0:1]
        block = jnp.zeros((2 * width, SIZE), jnp.float32)
        pick = iota((half, SIZE), 0) == iota((half, SIZE), 1) % width
        for k in range(kinds):
            place = jnp.where(pick & (jnp.abs(kind - k) < 0.5), 1.0, 0.0)
            block += lax.dot_general(
                bank_ref[k, :, :],
                place,
                (((0,), (0,)), ((), ())),
                precision=lax.Precision.HIGHEST,
                preferred_element_type=jnp.float32,
            )[: 2 * width]
        if 2 * width < 8:
            block = jnp.concatenate([block] * (8 // (2 * width)), axis=0)
        factor = jnp.concatenate([block] * (SIZE // block.shape[0]), axis=0)
        factor = jnp.where(row // (2 * width) == col // (2 * width), factor, 0.0)
        if product is None:
            product = factor
        else:
            product = jnp.dot(
                product, factor, precision=lax.Precision.HIGHEST, preferred_element_type=jnp.float32
            )
    return product


def far_first(turn):
    back = lax.rem(turn, 2)
    return SIDE // 2 + (1 - 2 * back) * lax.div(turn + back, 2)


def slot_of(group):
    y, z = lax.div(group, SIDE), lax.rem(group, SIDE)
    late, rest = lax.div(z, SIDE // 2), lax.rem(z, SIDE // 2)
    return ((late * 2 + lax.rem(rest, 2)) * QUARTER + lax.div(rest, 2)) * SIDE + y


def kernel(
    sino_any, bank_any, index_any, taps_any, out_ref,
    sino_ref, bank_ref, index_ref, taps_ref, send_buf, leaf_buf, result_buf, image_buf, tree_buf, early_buf,
    local_sem, leaf_send, leaf_recv, image_send, image_recv,
):
    views, columns = sino_ref.shape
    per_block = columns // LANES // BLOCKS
    window = per_block + 1
    slices = lax.axis_size("cuts")
    group = lax.axis_index("angle")
    cut = lax.axis_index("cuts")
    core = lax.rem(cut, CORES)
    first = cut - core
    here = [jnp.logical_and(group == y * SIDE + z, core == c) for y, z, c in OWNERS]
    is_owner = functools.reduce(jnp.logical_or, here)
    mine = sum(jnp.where(hit, b, 0) for b, hit in enumerate(here))
    late = lax.div(lax.rem(group, SIDE), SIDE // 2)

    has_side = [first > 0, True, True, first + CORES < slices]
    side_cut = [lax.rem(first + side - 1 + slices, slices) for side in range(4)]

    barrier = pltpu.get_barrier_semaphore()
    parts = [pl.ds(p * (columns // 2), columns // 2) for p in range(2)]
    sino_copies = [
        pltpu.make_async_copy(sino_any.at[:, part], sino_ref.at[:, part], local_sem.at[p])
        for p, part in enumerate(parts)
    ]
    for copy in sino_copies:
        copy.start()

    @pl.when(is_owner)
    def _():
        bank_copy = pltpu.make_async_copy(bank_any, bank_ref, local_sem.at[2])
        index_copy = pltpu.make_async_copy(index_any, index_ref, local_sem.at[3])
        taps_copy = pltpu.make_async_copy(taps_any, taps_ref, local_sem.at[4])
        bank_copy.start()
        index_copy.start()
        taps_copy.start()

        def announce(step, carry):
            y = lax.rem(lax.div(group, SIDE) + far_first(lax.rem(step, SIDE)), SIDE)
            z = lax.rem(group + far_first(lax.div(step, SIDE)), SIDE)
            target = y * SIDE + z
            for side in range(4):
                valid = has_side[side]
                if side in (1, 2):
                    valid = jnp.logical_or(target != group, core != side - 1)

                @pl.when(valid)
                def _():
                    pl.semaphore_signal(barrier, inc=1, device_id=(target, side_cut[side]), device_id_type=MESH)

            return carry

        lax.fori_loop(0, GROUPS, announce, 0)
        bank_copy.wait()
        index_copy.wait()
        taps_copy.wait()

    margin = jnp.zeros((1, LANES // 2), jnp.float32)
    pending = margin
    row = 0
    for part, copy in zip(parts, sino_copies):
        copy.wait()
        total = jnp.sum(sino_ref[:, part].astype(jnp.float32), axis=0, keepdims=True)
        if part is parts[-1]:
            total = jnp.concatenate([total, margin], axis=1)
        total = jnp.concatenate([pending, total], axis=1)
        for c in range(total.shape[1] // LANES):
            for b in range(BLOCKS):
                if 0 <= row - b * per_block < window:
                    send_buf[b, row - b * per_block : row - b * per_block + 1, :] = total[:, c * LANES : (c + 1) * LANES]
            row += 1
        pending = total[:, total.shape[1] // LANES * LANES :]

    has_other = jnp.where(core == 0, cut > 0, cut < slices - 1)
    other_first = lax.rem(jnp.where(core == 0, cut - CORES, cut + 1) + slices, slices)
    other_side = jnp.where(core == 0, 3, 0)
    n_owners = BLOCKS + jnp.where(has_other, BLOCKS, 0) - jnp.where(is_owner, 1, 0)
    pl.semaphore_wait(barrier, n_owners)

    def leaf_copy(b, turn):
        own = core != turn
        side = jnp.where(own, 1 + core, other_side)
        y, z, c = OWNERS[b]
        return pltpu.make_async_remote_copy(
            src_ref=send_buf.at[b],
            dst_ref=leaf_buf.at[side, slot_of(group)],
            send_sem=leaf_send,
            recv_sem=leaf_recv.at[side, late],
            device_id=(y * SIDE + z, jnp.where(own, first, other_first) + c),
            device_id_type=MESH,
        )

    for turn in range(2):
        valid = jnp.where(core != turn, True, has_other)

        @pl.when(jnp.logical_and(valid, jnp.logical_not(is_owner)))
        def _():
            for b in range(BLOCKS):
                leaf_copy(b, turn).start()

        @pl.when(jnp.logical_and(valid, is_owner))
        def _():
            for b in range(BLOCKS):

                @pl.when(jnp.logical_or(core == turn, mine != b))
                def _():
                    leaf_copy(b, turn).start()

    def all_left(count):
        sent = send_buf.at[pl.ds(0, count)]
        pltpu.make_async_copy(sent, sent, leaf_send).wait()

    pl.when(is_owner)(lambda: all_left(BLOCKS - 1))
    pl.when(jnp.logical_not(is_owner))(lambda: all_left(BLOCKS))
    pl.when(has_other)(lambda: all_left(BLOCKS))

    @pl.when(is_owner)
    def _():
        leaf_buf[1 + core, slot_of(group)] = send_buf[mine]
        row, col = iota((SIZE, SIZE), 0), iota((SIZE, SIZE), 1)
        place = lax.rem(col, HALF)
        z = (
            col // GROUPS * (SIDE // 2)
            + lax.rem(place // SIDE, QUARTER) * 2
            + place // (SIDE * QUARTER)
        )
        natural = 2 * (lax.rem(place, SIDE) * SIDE + z) + lax.rem(col // HALF, 2)
        order = (row == natural).astype(jnp.bfloat16)
        tree = tree_matrix(bank_ref, index_ref) * (1.0 / math.sqrt(views))
        high, low = [
            jnp.dot(part, order, preferred_element_type=jnp.float32).astype(jnp.bfloat16) for part in parts_of(tree)
        ]
        for part in range(2):
            span = slice(part * GROUPS, (part + 1) * GROUPS)
            tree_buf[part] = jnp.concatenate([high[:, span], low[:, span], high[:, span]], axis=1)

        lane, place = iota((HALF, LANES), 1), iota((HALF, LANES), 0)
        image = None
        for part in range(2):
            for side in range(4):
                def wait(count):
                    done = leaf_buf.at[side, pl.ds(0, count)]
                    pltpu.make_async_copy(done, done, leaf_recv.at[side, part]).wait()

                if side in (1, 2) and part == 0:
                    own = core == side - 1
                    pl.when(own)(lambda: wait(HALF - 1))
                    pl.when(jnp.logical_not(own))(lambda: wait(HALF))
                else:
                    pl.when(has_side[side])(lambda: wait(HALF))

            pair = lax.rem(place, SIDE) * (SIDE // 2) + lax.rem(place // SIDE, QUARTER) + part * QUARTER
            moved = [GROUPS // 4 - 1 - pair, pair - GROUPS // 4]
            back = lax.rem(lane - moved[0] + LANES // 2 + LANES, LANES)
            leaves = []
            for e in range(CORES):
                mixed = []
                for c in range(window):
                    term = None
                    for tap in range(3):
                        value = taps_ref[tap] * leaf_buf[e + tap, part * HALF : (part + 1) * HALF, c, :]
                        if e + tap in (0, 3):
                            value = jnp.where(has_side[e + tap], value, 0.0)
                        term = value if term is None else term + value
                    mixed.append(term)
                rows = []
                for r in range(2):
                    turned = []
                    for c in range(window):
                        if r == 0:
                            turned.append(jnp.take_along_axis(mixed[c], back, axis=1))
                            continue
                        pieces = []
                        for k in range(HALF // SIDE):
                            base = LANES // 2 - GROUPS // 4 + part * QUARTER + k % QUARTER
                            piece = mixed[c][k * SIDE : (k + 1) * SIDE]
                            pieces.append(pltpu.roll(piece, base, 1, stride=SIDE // 2, stride_axis=0))
                        turned.append(jnp.concatenate(pieces, axis=0))
                    rows.append(
                        jnp.concatenate(
                            [
                                jnp.where(lane - moved[r] < LANES // 2, turned[i], turned[i + 1])
                                for i in range(per_block)
                            ],
                            axis=1,
                        )
                    )
                leaves.append(jnp.concatenate(rows, axis=0))
            high, low = parts_of(jnp.concatenate(leaves, axis=1))
            product = jnp.dot(
                tree_buf[part], jnp.concatenate([high, high, low], axis=0), preferred_element_type=jnp.float32
            )
            if part == 0:
                early_buf[...] = product
            else:
                image = early_buf[...] + product
        for e in range(CORES):
            for i in range(per_block):
                start = (e * per_block + i) * LANES
                result_buf[e, :, i, :] = image[:, start : start + LANES]

        image_buf[pl.ds(2 * mine, 2)] = result_buf[core, pl.ds(2 * group, 2)]

        def give(step, carry):
            turn = lax.rem(step, SIDE)
            y = jnp.where(turn < SIDE // 2, turn, SIDE + SIDE // 2 - 1 - turn)
            target = y * SIDE + lax.div(step, SIDE)
            for e in range(CORES):

                @pl.when(jnp.logical_or(target != group, core != e))
                def _():
                    pltpu.make_async_remote_copy(
                        src_ref=result_buf.at[e, pl.ds(2 * target, 2)],
                        dst_ref=image_buf.at[pl.ds(2 * mine, 2)],
                        send_sem=image_send,
                        recv_sem=image_recv.at[mine],
                        device_id=(target, first + e),
                        device_id_type=MESH,
                    ).start()

            return carry

        lax.fori_loop(0, GROUPS, give, 0)

    for b in range(BLOCKS):
        got = image_buf.at[pl.ds(2 * b, 2)]

        @pl.when(jnp.logical_not(jnp.logical_and(is_owner, mine == b)))
        def _():
            pltpu.make_async_copy(got, got, image_recv.at[b]).wait()

        for i in range(per_block):
            c = b * per_block + i
            out_ref[:, c * LANES : (c + 1) * LANES] = image_buf[2 * b : 2 * b + 2, i, :]

    @pl.when(is_owner)
    def _():
        for e in range(CORES):
            own = core == e

            def wait(count):
                sent = result_buf.at[e, pl.ds(0, 2 * count)]
                pltpu.make_async_copy(sent, sent, image_send).wait()

            pl.when(own)(lambda: wait(GROUPS - 1))
            pl.when(jnp.logical_not(own))(lambda: wait(GROUPS))


def shards(sinogram, estimate, interp_bank, interp_index, slice_taps):
    _, views, columns = sinogram.shape
    per_block = columns // LANES // BLOCKS
    bank = jnp.swapaxes(interp_bank, 1, 2)
    operands = (sinogram[0], bank, interp_index.reshape(1, -1), slice_taps)
    held = [pltpu.with_memory_space_constraint(x, pltpu.HBM) for x in operands]
    mixed = pl.pallas_call(
        kernel,
        out_shape=pltpu.VMEM((2, columns), jnp.float32),
        in_specs=[pl.BlockSpec(memory_space=pltpu.HBM)] * 4,
        out_specs=pl.BlockSpec(memory_space=pltpu.VMEM),
        scratch_shapes=[
            pltpu.VMEM((views, columns), jnp.bfloat16),
            pltpu.VMEM(bank.shape, jnp.float32),
            pltpu.VMEM((1, SIZE), jnp.int32),
            pltpu.SMEM((3,), jnp.float32),
            pltpu.VMEM((BLOCKS, per_block + 1, LANES), jnp.float32),
            pltpu.VMEM((4, GROUPS, per_block + 1, LANES), jnp.float32),
            pltpu.VMEM((CORES, SIZE, per_block, LANES), jnp.float32),
            pltpu.VMEM((2 * BLOCKS, per_block, LANES), jnp.float32),
            pltpu.VMEM((2, SIZE, 3 * GROUPS), jnp.bfloat16),
            pltpu.VMEM((SIZE, CORES * columns // BLOCKS), jnp.float32),
            pltpu.SemaphoreType.DMA((5,)),
            pltpu.SemaphoreType.DMA,
            pltpu.SemaphoreType.DMA((4, 2)),
            pltpu.SemaphoreType.DMA,
            pltpu.SemaphoreType.DMA((BLOCKS,)),
        ],
        compiler_params=pltpu.CompilerParams(
            collective_id=0, has_side_effects=True, vmem_limit_bytes=32 * 1024 * 1024
        ),
    )(*held)
    return (estimate[0].astype(jnp.float32) - mixed)[None]


def solution(mesh):
    in_specs = (P("cuts", "angle", None), P("cuts", "angle", None), P(), P(), P())
    out_specs = P("cuts", "angle", None)
    return jax.shard_map(shards, mesh=mesh, in_specs=in_specs, out_specs=out_specs, check_vma=False)
```

```python
import functools
import math

import jax
import jax.numpy as jnp
from jax import lax
from jax.experimental import pallas as pl
from jax.experimental.pallas import tpu as pltpu
from jax.sharding import PartitionSpec as P

MESH = pl.DeviceIdType.MESH
SIDE = 8
CORES = 2
LANES = 128
GROUPS = SIDE * SIDE
SIZE = 2 * GROUPS
OWNERS = ((1, 0, 0), (1, 1, 1), (1, 1, 0), (2, 0, 0), (2, 0, 1), (7, 0, 0), (7, 0, 1), (6, 0, 0), (6, 0, 1), (3, 0, 0), (3, 0, 1), (5, 0, 0), (5, 0, 1), (0, 1, 0), (0, 1, 1), (4, 0, 0))
BLOCKS = len(OWNERS)
AHEAD = 2 * SIDE
QUARTER = SIDE // 4
HALF = GROUPS // 2


def parts_of(value):
    high = value.astype(jnp.bfloat16)
    low = (value - high.astype(jnp.float32)).astype(jnp.bfloat16)
    return high, low


def iota(shape, dim):
    return lax.broadcasted_iota(jnp.int32, shape, dim)


def tree_matrix(bank_ref, index_ref):
    kinds, half = bank_ref.shape[:2]
    levels = GROUPS.bit_length() - 1
    index = jnp.broadcast_to(index_ref[...].astype(jnp.float32), (8, SIZE))
    product = None
    for level in range(1, levels + 1):
        width = SIZE >> level
        row, col = iota((SIZE, SIZE), 0), iota((SIZE, SIZE), 1)
        chosen = (row == (1 << level) + col // width).astype(jnp.float32)
        kind = jnp.dot(index, chosen, preferred_element_type=jnp.float32)[0:1]
        block = jnp.zeros((2 * width, SIZE), jnp.float32)
        pick = iota((half, SIZE), 0) == iota((half, SIZE), 1) % width
        for k in range(kinds):
            place = jnp.where(pick & (jnp.abs(kind - k) < 0.5), 1.0, 0.0)
            block += lax.dot_general(
                bank_ref[k, :, :],
                place,
                (((0,), (0,)), ((), ())),
                precision=lax.Precision.HIGHEST,
                preferred_element_type=jnp.float32,
            )[: 2 * width]
        if 2 * width < 8:
            block = jnp.concatenate([block] * (8 // (2 * width)), axis=0)
        factor = jnp.concatenate([block] * (SIZE // block.shape[0]), axis=0)
        factor = jnp.where(row // (2 * width) == col // (2 * width), factor, 0.0)
        if product is None:
            product = factor
        else:
            product = jnp.dot(
                product, factor, precision=lax.Precision.HIGHEST, preferred_element_type=jnp.float32
            )
    return product


def far_first(turn):
    back = lax.rem(turn, 2)
    return SIDE // 2 + (1 - 2 * back) * lax.div(turn + back, 2)


def slot_of(group):
    y, z = lax.div(group, SIDE), lax.rem(group, SIDE)
    late, rest = lax.div(z, SIDE // 2), lax.rem(z, SIDE // 2)
    return ((late * 2 + lax.rem(rest, 2)) * QUARTER + lax.div(rest, 2)) * SIDE + y


def kernel(
    sino_any, bank_any, index_any, taps_any, out_ref,
    sino_ref, bank_ref, index_ref, taps_ref, send_buf, leaf_buf, result_buf, image_buf, tree_buf, early_buf,
    local_sem, leaf_send, leaf_recv, image_send, image_recv,
):
    views, columns = sino_ref.shape
    per_block = columns // LANES // BLOCKS
    window = per_block + 1
    slices = lax.axis_size("cuts")
    group = lax.axis_index("angle")
    cut = lax.axis_index("cuts")
    core = lax.rem(cut, CORES)
    first = cut - core
    here = [jnp.logical_and(group == y * SIDE + z, core == c) for y, z, c in OWNERS]
    is_owner = functools.reduce(jnp.logical_or, here)
    mine = sum(jnp.where(hit, b, 0) for b, hit in enumerate(here))
    late = lax.div(lax.rem(group, SIDE), SIDE // 2)

    has_side = [first > 0, True, True, first + CORES < slices]
    side_cut = [lax.rem(first + side - 1 + slices, slices) for side in range(4)]

    barrier = pltpu.get_barrier_semaphore()
    parts = [pl.ds(p * (columns // 2), columns // 2) for p in range(2)]
    sino_copies = [
        pltpu.make_async_copy(sino_any.at[:, part], sino_ref.at[:, part], local_sem.at[p])
        for p, part in enumerate(parts)
    ]
    for copy in sino_copies:
        copy.start()

    @pl.when(is_owner)
    def _():
        bank_copy = pltpu.make_async_copy(bank_any, bank_ref, local_sem.at[2])
        index_copy = pltpu.make_async_copy(index_any, index_ref, local_sem.at[3])
        taps_copy = pltpu.make_async_copy(taps_any, taps_ref, local_sem.at[4])
        bank_copy.start()
        index_copy.start()
        taps_copy.start()

        def announce(step, carry):
            y = lax.rem(lax.div(group, SIDE) + far_first(lax.rem(step, SIDE)), SIDE)
            z = lax.rem(group + far_first(lax.div(step, SIDE)), SIDE)
            target = y * SIDE + z
            for side in range(4):
                valid = has_side[side]
                if side in (1, 2):
                    valid = jnp.logical_or(target != group, core != side - 1)

                @pl.when(valid)
                def _():
                    pl.semaphore_signal(barrier, inc=1, device_id=(target, side_cut[side]), device_id_type=MESH)

            return carry

        lax.fori_loop(0, GROUPS, announce, 0)
        bank_copy.wait()
        index_copy.wait()
        taps_copy.wait()

    margin = jnp.zeros((1, LANES // 2), jnp.float32)
    pending = margin
    row = 0
    for part, copy in zip(parts, sino_copies):
        copy.wait()
        total = jnp.sum(sino_ref[:, part].astype(jnp.float32), axis=0, keepdims=True)
        if part is parts[-1]:
            total = jnp.concatenate([total, margin], axis=1)
        total = jnp.concatenate([pending, total], axis=1)
        for c in range(total.shape[1] // LANES):
            for b in range(BLOCKS):
                if 0 <= row - b * per_block < window:
                    send_buf[b, row - b * per_block : row - b * per_block + 1, :] = total[:, c * LANES : (c + 1) * LANES]
            row += 1
        pending = total[:, total.shape[1] // LANES * LANES :]

    has_other = jnp.where(core == 0, cut > 0, cut < slices - 1)
    other_first = lax.rem(jnp.where(core == 0, cut - CORES, cut + 1) + slices, slices)
    other_side = jnp.where(core == 0, 3, 0)
    n_owners = BLOCKS + jnp.where(has_other, BLOCKS, 0) - jnp.where(is_owner, 1, 0)
    pl.semaphore_wait(barrier, n_owners)

    def leaf_copy(b, turn):
        own = core != turn
        side = jnp.where(own, 1 + core, other_side)
        y, z, c = OWNERS[b]
        return pltpu.make_async_remote_copy(
            src_ref=send_buf.at[b],
            dst_ref=leaf_buf.at[side, slot_of(group)],
            send_sem=leaf_send,
            recv_sem=leaf_recv.at[side, late],
            device_id=(y * SIDE + z, jnp.where(own, first, other_first) + c),
            device_id_type=MESH,
        )

    for turn in range(2):
        valid = jnp.where(core != turn, True, has_other)

        @pl.when(jnp.logical_and(valid, jnp.logical_not(is_owner)))
        def _():
            for b in range(BLOCKS):
                leaf_copy(b, turn).start()

        @pl.when(jnp.logical_and(valid, is_owner))
        def _():
            for b in range(BLOCKS):

                @pl.when(jnp.logical_or(core == turn, mine != b))
                def _():
                    leaf_copy(b, turn).start()

    def all_left(count):
        sent = send_buf.at[pl.ds(0, count)]
        pltpu.make_async_copy(sent, sent, leaf_send).wait()

    pl.when(is_owner)(lambda: all_left(BLOCKS - 1))
    pl.when(jnp.logical_not(is_owner))(lambda: all_left(BLOCKS))
    pl.when(has_other)(lambda: all_left(BLOCKS))

    @pl.when(is_owner)
    def _():
        leaf_buf[1 + core, slot_of(group)] = send_buf[mine]
        row, col = iota((SIZE, SIZE), 0), iota((SIZE, SIZE), 1)
        place = lax.rem(col, HALF)
        z = (
            col // GROUPS * (SIDE // 2)
            + lax.rem(place // SIDE, QUARTER) * 2
            + place // (SIDE * QUARTER)
        )
        natural = 2 * (lax.rem(place, SIDE) * SIDE + z) + lax.rem(col // HALF, 2)
        order = (row == natural).astype(jnp.bfloat16)
        tree = tree_matrix(bank_ref, index_ref) * (1.0 / math.sqrt(views))
        high, low = [
            jnp.dot(part, order, preferred_element_type=jnp.float32).astype(jnp.bfloat16) for part in parts_of(tree)
        ]
        for part in range(2):
            span = slice(part * GROUPS, (part + 1) * GROUPS)
            tree_buf[part] = jnp.concatenate([high[:, span], low[:, span], high[:, span]], axis=1)

        lane, place = iota((HALF, LANES), 1), iota((HALF, LANES), 0)

        def arrived(side, part):
            def wait(count):
                done = leaf_buf.at[side, pl.ds(0, count)]
                pltpu.make_async_copy(done, done, leaf_recv.at[side, part]).wait()

            if side in (1, 2) and part == 0:
                own = core == side - 1
                pl.when(own)(lambda: wait(HALF - 1))
                pl.when(jnp.logical_not(own))(lambda: wait(HALF))
            else:
                pl.when(has_side[side])(lambda: wait(HALF))

        def merged(part, terms):
            pair = lax.rem(place, SIDE) * (SIDE // 2) + lax.rem(place // SIDE, QUARTER) + part * QUARTER
            moved = [GROUPS // 4 - 1 - pair, pair - GROUPS // 4]
            back = lax.rem(lane - moved[0] + LANES // 2 + LANES, LANES)
            mixed = []
            for c in range(window):
                total = None
                for tap, side in terms:
                    value = taps_ref[tap] * leaf_buf[side, part * HALF : (part + 1) * HALF, c, :]
                    if side in (0, 3):
                        value = jnp.where(has_side[side], value, 0.0)
                    total = value if total is None else total + value
                mixed.append(total)
            rows = []
            for r in range(2):
                turned = []
                for c in range(window):
                    if r == 0:
                        turned.append(jnp.take_along_axis(mixed[c], back, axis=1))
                        continue
                    pieces = []
                    for k in range(HALF // SIDE):
                        base = LANES // 2 - GROUPS // 4 + part * QUARTER + k % QUARTER
                        piece = mixed[c][k * SIDE : (k + 1) * SIDE]
                        pieces.append(pltpu.roll(piece, base, 1, stride=SIDE // 2, stride_axis=0))
                    turned.append(jnp.concatenate(pieces, axis=0))
                rows.append(
                    jnp.concatenate(
                        [jnp.where(lane - moved[r] < LANES // 2, turned[i], turned[i + 1]) for i in range(per_block)],
                        axis=1,
                    )
                )
            high, low = parts_of(jnp.concatenate(rows, axis=0))
            return jnp.dot(
                tree_buf[part], jnp.concatenate([high, high, low], axis=0), preferred_element_type=jnp.float32
            )

        def keep(e, image):
            for i in range(per_block):
                result_buf[e, :, i, :] = image[:, i * LANES : (i + 1) * LANES]

        def give(e, step):
            turn = lax.rem(step, SIDE)
            y = jnp.where(turn < SIDE // 2, turn, SIDE + SIDE // 2 - 1 - turn)
            target = y * SIDE + lax.div(step, SIDE)

            @pl.when(jnp.logical_or(target != group, core != e))
            def _():
                pltpu.make_async_remote_copy(
                    src_ref=result_buf.at[e, pl.ds(2 * target, 2)],
                    dst_ref=image_buf.at[pl.ds(2 * mine, 2)],
                    send_sem=image_send,
                    recv_sem=image_recv.at[mine],
                    device_id=(target, first + e),
                    device_id_type=MESH,
                ).start()

        def give_all(start, stop, which):
            def body(step, carry):
                for e in which:
                    give(e, step)
                return carry

            lax.fori_loop(start, stop, body, 0)

        for side in range(4):
            arrived(side, 0)
        early_buf[0] = merged(0, [(0, 0), (1, 1), (2, 2)])
        early_buf[1] = merged(0, [(0, 1), (1, 2), (2, 3)])
        for side in range(3):
            arrived(side, 1)
        keep(0, early_buf[0] + merged(1, [(0, 0), (1, 1), (2, 2)]))
        give_all(0, AHEAD, (0,))
        early_buf[1] += merged(1, [(0, 1), (1, 2)])
        arrived(3, 1)
        keep(1, early_buf[1] + merged(1, [(2, 3)]))
        give_all(0, AHEAD, (1,))
        give_all(AHEAD, GROUPS, (0, 1))
        image_buf[pl.ds(2 * mine, 2)] = result_buf[core, pl.ds(2 * group, 2)]

    for b in range(BLOCKS):
        got = image_buf.at[pl.ds(2 * b, 2)]

        @pl.when(jnp.logical_not(jnp.logical_and(is_owner, mine == b)))
        def _():
            pltpu.make_async_copy(got, got, image_recv.at[b]).wait()

        for i in range(per_block):
            c = b * per_block + i
            out_ref[:, c * LANES : (c + 1) * LANES] = image_buf[2 * b : 2 * b + 2, i, :]

    @pl.when(is_owner)
    def _():
        for e in range(CORES):
            own = core == e

            def wait(count):
                sent = result_buf.at[e, pl.ds(0, 2 * count)]
                pltpu.make_async_copy(sent, sent, image_send).wait()

            pl.when(own)(lambda: wait(GROUPS - 1))
            pl.when(jnp.logical_not(own))(lambda: wait(GROUPS))


def shards(sinogram, estimate, interp_bank, interp_index, slice_taps):
    _, views, columns = sinogram.shape
    per_block = columns // LANES // BLOCKS
    bank = jnp.swapaxes(interp_bank, 1, 2)
    operands = (sinogram[0], bank, interp_index.reshape(1, -1), slice_taps)
    held = [pltpu.with_memory_space_constraint(x, pltpu.HBM) for x in operands]
    mixed = pl.pallas_call(
        kernel,
        out_shape=pltpu.VMEM((2, columns), jnp.float32),
        in_specs=[pl.BlockSpec(memory_space=pltpu.HBM)] * 4,
        out_specs=pl.BlockSpec(memory_space=pltpu.VMEM),
        scratch_shapes=[
            pltpu.VMEM((views, columns), jnp.bfloat16),
            pltpu.VMEM(bank.shape, jnp.float32),
            pltpu.VMEM((1, SIZE), jnp.int32),
            pltpu.SMEM((3,), jnp.float32),
            pltpu.VMEM((BLOCKS, per_block + 1, LANES), jnp.float32),
            pltpu.VMEM((4, GROUPS, per_block + 1, LANES), jnp.float32),
            pltpu.VMEM((CORES, SIZE, per_block, LANES), jnp.float32),
            pltpu.VMEM((2 * BLOCKS, per_block, LANES), jnp.float32),
            pltpu.VMEM((2, SIZE, 3 * GROUPS), jnp.bfloat16),
            pltpu.VMEM((CORES, SIZE, columns // BLOCKS), jnp.float32),
            pltpu.SemaphoreType.DMA((5,)),
            pltpu.SemaphoreType.DMA,
            pltpu.SemaphoreType.DMA((4, 2)),
            pltpu.SemaphoreType.DMA,
            pltpu.SemaphoreType.DMA((BLOCKS,)),
        ],
        compiler_params=pltpu.CompilerParams(
            collective_id=0, has_side_effects=True, vmem_limit_bytes=32 * 1024 * 1024
        ),
    )(*held)
    return (estimate[0].astype(jnp.float32) - mixed)[None]


def solution(mesh):
    in_specs = (P("cuts", "angle", None), P("cuts", "angle", None), P(), P(), P())
    out_specs = P("cuts", "angle", None)
    return jax.shard_map(shards, mesh=mesh, in_specs=in_specs, out_specs=out_specs, check_vma=False)
```

```python
import functools
import math

import jax
import jax.numpy as jnp
from jax import lax
from jax.experimental import pallas as pl
from jax.experimental.pallas import tpu as pltpu
from jax.sharding import PartitionSpec as P

MESH = pl.DeviceIdType.MESH
SIDE = 8
CORES = 2
LANES = 128
GROUPS = SIDE * SIDE
SIZE = 2 * GROUPS
OWNERS = ((0, 1, 0), (0, 1, 1), (1, 1, 0), (1, 1, 1), (4, 0, 0), (1, 0, 0), (2, 0, 0), (2, 0, 1), (7, 0, 0), (7, 0, 1), (6, 0, 0), (6, 0, 1), (3, 0, 0), (3, 0, 1), (5, 0, 0), (5, 0, 1))
BLOCKS = len(OWNERS)
AHEAD, LEAD = 10, 2
QUARTER = SIDE // 4
HALF = GROUPS // 2


def parts_of(value):
    high = value.astype(jnp.bfloat16)
    low = (value - high.astype(jnp.float32)).astype(jnp.bfloat16)
    return high, low


def iota(shape, dim):
    return lax.broadcasted_iota(jnp.int32, shape, dim)


def tree_matrix(bank_ref, index_ref):
    kinds, half = bank_ref.shape[:2]
    levels = GROUPS.bit_length() - 1
    index = jnp.broadcast_to(index_ref[...].astype(jnp.float32), (8, SIZE))
    product = None
    for level in range(1, levels + 1):
        width = SIZE >> level
        row, col = iota((SIZE, SIZE), 0), iota((SIZE, SIZE), 1)
        chosen = (row == (1 << level) + col // width).astype(jnp.float32)
        kind = jnp.dot(index, chosen, preferred_element_type=jnp.float32)[0:1]
        block = jnp.zeros((2 * width, SIZE), jnp.float32)
        pick = iota((half, SIZE), 0) == iota((half, SIZE), 1) % width
        for k in range(kinds):
            place = jnp.where(pick & (jnp.abs(kind - k) < 0.5), 1.0, 0.0)
            block += lax.dot_general(
                bank_ref[k, :, :],
                place,
                (((0,), (0,)), ((), ())),
                precision=lax.Precision.HIGHEST,
                preferred_element_type=jnp.float32,
            )[: 2 * width]
        if 2 * width < 8:
            block = jnp.concatenate([block] * (8 // (2 * width)), axis=0)
        factor = jnp.concatenate([block] * (SIZE // block.shape[0]), axis=0)
        factor = jnp.where(row // (2 * width) == col // (2 * width), factor, 0.0)
        if product is None:
            product = factor
        else:
            product = jnp.dot(
                product, factor, precision=lax.Precision.HIGHEST, preferred_element_type=jnp.float32
            )
    return product


def far_first(turn):
    back = lax.rem(turn, 2)
    return SIDE // 2 + (1 - 2 * back) * lax.div(turn + back, 2)


def slot_of(group):
    y, z = lax.div(group, SIDE), lax.rem(group, SIDE)
    late, rest = lax.div(z, SIDE // 2), lax.rem(z, SIDE // 2)
    return ((late * 2 + lax.rem(rest, 2)) * QUARTER + lax.div(rest, 2)) * SIDE + y


def kernel(
    sino_any, bank_any, index_any, taps_any, out_ref,
    sino_ref, bank_ref, index_ref, taps_ref, send_buf, leaf_buf, result_buf, image_buf, tree_buf, early_buf,
    local_sem, leaf_send, leaf_recv, image_send, image_recv,
):
    views, columns = sino_ref.shape
    per_block = columns // LANES // BLOCKS
    window = per_block + 1
    slices = lax.axis_size("cuts")
    group = lax.axis_index("angle")
    cut = lax.axis_index("cuts")
    core = lax.rem(cut, CORES)
    first = cut - core
    here = [jnp.logical_and(group == y * SIDE + z, core == c) for y, z, c in OWNERS]
    is_owner = functools.reduce(jnp.logical_or, here)
    mine = sum(jnp.where(hit, b, 0) for b, hit in enumerate(here))
    late = lax.div(lax.rem(group, SIDE), SIDE // 2)

    has_side = [first > 0, True, True, first + CORES < slices]
    side_cut = [lax.rem(first + side - 1 + slices, slices) for side in range(4)]

    barrier = pltpu.get_barrier_semaphore()
    sino_copy = pltpu.make_async_copy(sino_any, sino_ref, local_sem.at[0])
    sino_copy.start()

    @pl.when(is_owner)
    def _():
        bank_copy = pltpu.make_async_copy(bank_any, bank_ref, local_sem.at[1])
        index_copy = pltpu.make_async_copy(index_any, index_ref, local_sem.at[2])
        taps_copy = pltpu.make_async_copy(taps_any, taps_ref, local_sem.at[3])
        bank_copy.start()
        index_copy.start()
        taps_copy.start()

        def announce(step, carry):
            y = lax.rem(lax.div(group, SIDE) + far_first(lax.rem(step, SIDE)), SIDE)
            z = lax.rem(group + far_first(lax.div(step, SIDE)), SIDE)
            target = y * SIDE + z
            for side in range(4):
                valid = has_side[side]
                if side in (1, 2):
                    valid = jnp.logical_or(target != group, core != side - 1)

                @pl.when(valid)
                def _():
                    pl.semaphore_signal(barrier, inc=1, device_id=(target, side_cut[side]), device_id_type=MESH)

            return carry

        lax.fori_loop(0, GROUPS, announce, 0)
        bank_copy.wait()
        index_copy.wait()
        taps_copy.wait()

    sino_copy.wait()
    total = jnp.sum(sino_ref[...].astype(jnp.float32), axis=0, keepdims=True)
    margin = jnp.zeros((1, LANES // 2), jnp.float32)
    total = jnp.concatenate([margin, total, margin], axis=1)
    for b in range(BLOCKS):
        for c in range(window):
            start = (b * per_block + c) * LANES
            send_buf[b, c : c + 1, :] = total[:, start : start + LANES]

    has_other = jnp.where(core == 0, cut > 0, cut < slices - 1)
    other_first = lax.rem(jnp.where(core == 0, cut - CORES, cut + 1) + slices, slices)
    other_side = jnp.where(core == 0, 3, 0)
    n_owners = BLOCKS + jnp.where(has_other, BLOCKS, 0) - jnp.where(is_owner, 1, 0)
    pl.semaphore_wait(barrier, n_owners)

    def leaf_copy(b, turn):
        own = core != turn
        side = jnp.where(own, 1 + core, other_side)
        y, z, c = OWNERS[b]
        return pltpu.make_async_remote_copy(
            src_ref=send_buf.at[b],
            dst_ref=leaf_buf.at[side, slot_of(group)],
            send_sem=leaf_send,
            recv_sem=leaf_recv.at[side, late],
            device_id=(y * SIDE + z, jnp.where(own, first, other_first) + c),
            device_id_type=MESH,
        )

    for turn in range(2):
        valid = jnp.where(core != turn, True, has_other)

        @pl.when(jnp.logical_and(valid, jnp.logical_not(is_owner)))
        def _():
            for b in range(BLOCKS):
                leaf_copy(b, turn).start()

        @pl.when(jnp.logical_and(valid, is_owner))
        def _():
            for b in range(BLOCKS):

                @pl.when(jnp.logical_or(core == turn, mine != b))
                def _():
                    leaf_copy(b, turn).start()

    def all_left(count):
        sent = send_buf.at[pl.ds(0, count)]
        pltpu.make_async_copy(sent, sent, leaf_send).wait()

    pl.when(is_owner)(lambda: all_left(BLOCKS - 1))
    pl.when(jnp.logical_not(is_owner))(lambda: all_left(BLOCKS))
    pl.when(has_other)(lambda: all_left(BLOCKS))

    @pl.when(is_owner)
    def _():
        leaf_buf[1 + core, slot_of(group)] = send_buf[mine]
        row, col = iota((SIZE, SIZE), 0), iota((SIZE, SIZE), 1)
        place = lax.rem(col, HALF)
        z = (
            col // GROUPS * (SIDE // 2)
            + lax.rem(place // SIDE, QUARTER) * 2
            + place // (SIDE * QUARTER)
        )
        natural = 2 * (lax.rem(place, SIDE) * SIDE + z) + lax.rem(col // HALF, 2)
        order = (row == natural).astype(jnp.bfloat16)
        tree = tree_matrix(bank_ref, index_ref) * (1.0 / math.sqrt(views))
        high, low = [
            jnp.dot(part, order, preferred_element_type=jnp.float32).astype(jnp.bfloat16) for part in parts_of(tree)
        ]
        for part in range(2):
            span = slice(part * GROUPS, (part + 1) * GROUPS)
            tree_buf[part] = jnp.concatenate([high[:, span], low[:, span], high[:, span]], axis=1)

        lane, place = iota((HALF, LANES), 1), iota((HALF, LANES), 0)

        def arrived(side, part):
            def wait(count):
                done = leaf_buf.at[side, pl.ds(0, count)]
                pltpu.make_async_copy(done, done, leaf_recv.at[side, part]).wait()

            if side in (1, 2) and part == 0:
                own = core == side - 1
                pl.when(own)(lambda: wait(HALF - 1))
                pl.when(jnp.logical_not(own))(lambda: wait(HALF))
            else:
                pl.when(has_side[side])(lambda: wait(HALF))

        def merged(part, terms):
            pair = lax.rem(place, SIDE) * (SIDE // 2) + lax.rem(place // SIDE, QUARTER) + part * QUARTER
            moved = [GROUPS // 4 - 1 - pair, pair - GROUPS // 4]
            back = lax.rem(lane - moved[0] + LANES // 2 + LANES, LANES)
            mixed = []
            for c in range(window):
                total = None
                for tap, side in terms:
                    value = taps_ref[tap] * leaf_buf[side, part * HALF : (part + 1) * HALF, c, :]
                    if side in (0, 3):
                        value = jnp.where(has_side[side], value, 0.0)
                    total = value if total is None else total + value
                mixed.append(total)
            rows = []
            for r in range(2):
                turned = []
                for c in range(window):
                    if r == 0:
                        turned.append(jnp.take_along_axis(mixed[c], back, axis=1))
                        continue
                    pieces = []
                    for k in range(HALF // SIDE):
                        base = LANES // 2 - GROUPS // 4 + part * QUARTER + k % QUARTER
                        piece = mixed[c][k * SIDE : (k + 1) * SIDE]
                        pieces.append(pltpu.roll(piece, base, 1, stride=SIDE // 2, stride_axis=0))
                    turned.append(jnp.concatenate(pieces, axis=0))
                rows.append(
                    jnp.concatenate(
                        [jnp.where(lane - moved[r] < LANES // 2, turned[i], turned[i + 1]) for i in range(per_block)],
                        axis=1,
                    )
                )
            high, low = parts_of(jnp.concatenate(rows, axis=0))
            return jnp.dot(
                tree_buf[part], jnp.concatenate([high, high, low], axis=0), preferred_element_type=jnp.float32
            )

        def keep(e, image):
            for i in range(per_block):
                result_buf[e, :, i, :] = image[:, i * LANES : (i + 1) * LANES]

        def give(e, step):
            turn = lax.rem(step, SIDE)
            y = jnp.where(turn < SIDE // 2, turn, SIDE + SIDE // 2 - 1 - turn)
            target = y * SIDE + lax.div(step, SIDE)

            @pl.when(jnp.logical_or(target != group, core != e))
            def _():
                pltpu.make_async_remote_copy(
                    src_ref=result_buf.at[e, pl.ds(2 * target, 2)],
                    dst_ref=image_buf.at[pl.ds(2 * mine, 2)],
                    send_sem=image_send,
                    recv_sem=image_recv.at[mine],
                    device_id=(target, first + e),
                    device_id_type=MESH,
                ).start()

        def give_all(start, stop, which):
            def body(step, carry):
                for e in which:
                    give(e, step)
                return carry

            lax.fori_loop(start, stop, body, 0)

        for side in range(4):
            arrived(side, 0)
        early_buf[0] = merged(0, [(0, 0), (1, 1), (2, 2)])
        early_buf[1] = merged(0, [(0, 1), (1, 2), (2, 3)])
        for side in range(3):
            arrived(side, 1)
        keep(0, early_buf[0] + merged(1, [(0, 0), (1, 1), (2, 2)]))
        give_all(0, AHEAD, (0,))
        early_buf[1] += merged(1, [(0, 1), (1, 2)])
        arrived(3, 1)
        keep(1, early_buf[1] + merged(1, [(2, 3)]))
        give_all(0, AHEAD + LEAD, (1,))

        def give_both(step, carry):
            give(0, step)
            give(1, step + LEAD)
            return carry

        lax.fori_loop(AHEAD, GROUPS - LEAD, give_both, 0)
        give_all(GROUPS - LEAD, GROUPS, (0,))
        image_buf[pl.ds(2 * mine, 2)] = result_buf[core, pl.ds(2 * group, 2)]

    for b in range(BLOCKS):
        got = image_buf.at[pl.ds(2 * b, 2)]

        @pl.when(jnp.logical_not(jnp.logical_and(is_owner, mine == b)))
        def _():
            pltpu.make_async_copy(got, got, image_recv.at[b]).wait()

        for i in range(per_block):
            c = b * per_block + i
            out_ref[:, c * LANES : (c + 1) * LANES] = image_buf[2 * b : 2 * b + 2, i, :]

    @pl.when(is_owner)
    def _():
        for e in range(CORES):
            own = core == e

            def wait(count):
                sent = result_buf.at[e, pl.ds(0, 2 * count)]
                pltpu.make_async_copy(sent, sent, image_send).wait()

            pl.when(own)(lambda: wait(GROUPS - 1))
            pl.when(jnp.logical_not(own))(lambda: wait(GROUPS))


def shards(sinogram, estimate, interp_bank, interp_index, slice_taps):
    _, views, columns = sinogram.shape
    per_block = columns // LANES // BLOCKS
    bank = jnp.swapaxes(interp_bank, 1, 2)
    operands = (sinogram[0], bank, interp_index.reshape(1, -1), slice_taps)
    held = [pltpu.with_memory_space_constraint(x, pltpu.HBM) for x in operands]
    mixed = pl.pallas_call(
        kernel,
        out_shape=pltpu.VMEM((2, columns), jnp.float32),
        in_specs=[pl.BlockSpec(memory_space=pltpu.HBM)] * 4,
        out_specs=pl.BlockSpec(memory_space=pltpu.VMEM),
        scratch_shapes=[
            pltpu.VMEM((views, columns), jnp.bfloat16),
            pltpu.VMEM(bank.shape, jnp.float32),
            pltpu.VMEM((1, SIZE), jnp.int32),
            pltpu.SMEM((3,), jnp.float32),
            pltpu.VMEM((BLOCKS, per_block + 1, LANES), jnp.float32),
            pltpu.VMEM((4, GROUPS, per_block + 1, LANES), jnp.float32),
            pltpu.VMEM((CORES, SIZE, per_block, LANES), jnp.float32),
            pltpu.VMEM((2 * BLOCKS, per_block, LANES), jnp.float32),
            pltpu.VMEM((2, SIZE, 3 * GROUPS), jnp.bfloat16),
            pltpu.VMEM((CORES, SIZE, columns // BLOCKS), jnp.float32),
            pltpu.SemaphoreType.DMA((4,)),
            pltpu.SemaphoreType.DMA,
            pltpu.SemaphoreType.DMA((4, 2)),
            pltpu.SemaphoreType.DMA,
            pltpu.SemaphoreType.DMA((BLOCKS,)),
        ],
        compiler_params=pltpu.CompilerParams(
            collective_id=0, has_side_effects=True, vmem_limit_bytes=32 * 1024 * 1024
        ),
    )(*held)
    return (estimate[0].astype(jnp.float32) - mixed)[None]


def solution(mesh):
    in_specs = (P("cuts", "angle", None), P("cuts", "angle", None), P(), P(), P())
    out_specs = P("cuts", "angle", None)
    return jax.shard_map(shards, mesh=mesh, in_specs=in_specs, out_specs=out_specs, check_vma=False)
```

```python
import functools
import math

import jax
import jax.numpy as jnp
from jax import lax
from jax.experimental import pallas as pl
from jax.experimental.pallas import tpu as pltpu
from jax.sharding import PartitionSpec as P

MESH = pl.DeviceIdType.MESH
SIDE = 8
CORES = 2
LANES = 128
GROUPS = SIDE * SIDE
SIZE = 2 * GROUPS
OWNERS = ((0, 1, 0), (0, 1, 1), (1, 1, 0), (1, 1, 1), (4, 0, 0), (1, 0, 0), (2, 0, 0), (2, 0, 1), (7, 0, 0), (7, 0, 1), (6, 0, 0), (6, 0, 1), (3, 0, 0), (3, 0, 1), (5, 0, 0), (5, 0, 1))
BLOCKS = len(OWNERS)
AHEAD, LEAD = 10, 2
QUARTER = SIDE // 4
HALF = GROUPS // 2


def parts_of(value):
    high = value.astype(jnp.bfloat16)
    low = (value - high.astype(jnp.float32)).astype(jnp.bfloat16)
    return high, low


def iota(shape, dim):
    return lax.broadcasted_iota(jnp.int32, shape, dim)


def tree_matrix(bank_ref, index_ref):
    kinds, half = bank_ref.shape[:2]
    levels = GROUPS.bit_length() - 1
    index = jnp.broadcast_to(index_ref[...].astype(jnp.float32), (8, SIZE))
    product = None
    for level in range(1, levels + 1):
        width = SIZE >> level
        row, col = iota((SIZE, SIZE), 0), iota((SIZE, SIZE), 1)
        chosen = (row == (1 << level) + col // width).astype(jnp.float32)
        kind = jnp.dot(index, chosen, preferred_element_type=jnp.float32)[0:1]
        block = jnp.zeros((2 * width, SIZE), jnp.float32)
        pick = iota((half, SIZE), 0) == iota((half, SIZE), 1) % width
        for k in range(kinds):
            place = jnp.where(pick & (jnp.abs(kind - k) < 0.5), 1.0, 0.0)
            block += lax.dot_general(
                bank_ref[k, :, :],
                place,
                (((0,), (0,)), ((), ())),
                precision=lax.Precision.HIGHEST,
                preferred_element_type=jnp.float32,
            )[: 2 * width]
        if 2 * width < 8:
            block = jnp.concatenate([block] * (8 // (2 * width)), axis=0)
        factor = jnp.concatenate([block] * (SIZE // block.shape[0]), axis=0)
        factor = jnp.where(row // (2 * width) == col // (2 * width), factor, 0.0)
        if product is None:
            product = factor
        else:
            product = jnp.dot(
                product, factor, precision=lax.Precision.HIGHEST, preferred_element_type=jnp.float32
            )
    return product


def far_first(turn):
    back = lax.rem(turn, 2)
    return SIDE // 2 + (1 - 2 * back) * lax.div(turn + back, 2)


def slot_of(group):
    y, z = lax.div(group, SIDE), lax.rem(group, SIDE)
    late, rest = lax.div(z, SIDE // 2), lax.rem(z, SIDE // 2)
    return ((late * 2 + lax.rem(rest, 2)) * QUARTER + lax.div(rest, 2)) * SIDE + y


def kernel(
    sino_any, bank_any, index_any, taps_any, out_ref,
    sino_ref, bank_ref, index_ref, taps_ref, send_buf, leaf_buf, result_buf, image_buf, tree_buf, early_buf,
    local_sem, leaf_send, leaf_recv, image_send, image_recv,
):
    views, columns = sino_ref.shape
    per_block = columns // LANES // BLOCKS
    window = per_block + 1
    slices = lax.axis_size("cuts")
    group = lax.axis_index("angle")
    cut = lax.axis_index("cuts")
    core = lax.rem(cut, CORES)
    first = cut - core
    here = [jnp.logical_and(group == y * SIDE + z, core == c) for y, z, c in OWNERS]
    is_owner = functools.reduce(jnp.logical_or, here)
    mine = sum(jnp.where(hit, b, 0) for b, hit in enumerate(here))
    late = lax.div(lax.rem(group, SIDE), SIDE // 2)

    has_side = [first > 0, True, True, first + CORES < slices]
    side_cut = [lax.rem(first + side - 1 + slices, slices) for side in range(4)]

    barrier = pltpu.get_barrier_semaphore()
    sino_copy = pltpu.make_async_copy(sino_any, sino_ref, local_sem.at[0])
    sino_copy.start()

    @pl.when(is_owner)
    def _():
        bank_copy = pltpu.make_async_copy(bank_any, bank_ref, local_sem.at[1])
        index_copy = pltpu.make_async_copy(index_any, index_ref, local_sem.at[2])
        taps_copy = pltpu.make_async_copy(taps_any, taps_ref, local_sem.at[3])
        bank_copy.start()
        index_copy.start()
        taps_copy.start()

        def announce(step, carry):
            y = lax.rem(lax.div(group, SIDE) + far_first(lax.rem(step, SIDE)), SIDE)
            z = lax.rem(group + far_first(lax.div(step, SIDE)), SIDE)
            target = y * SIDE + z
            for side in range(4):
                valid = has_side[side]
                if side in (1, 2):
                    valid = jnp.logical_or(target != group, core != side - 1)

                @pl.when(valid)
                def _():
                    pl.semaphore_signal(barrier, inc=1, device_id=(target, side_cut[side]), device_id_type=MESH)

            return carry

        lax.fori_loop(0, GROUPS, announce, 0)
        bank_copy.wait()
        index_copy.wait()
        taps_copy.wait()

    sino_copy.wait()
    total = jnp.sum(sino_ref[...].astype(jnp.float32), axis=0, keepdims=True)
    margin = jnp.zeros((1, LANES // 2), jnp.float32)
    total = jnp.concatenate([margin, total, margin], axis=1)
    for b in range(BLOCKS):
        for c in range(window):
            start = (b * per_block + c) * LANES
            send_buf[b, c : c + 1, :] = total[:, start : start + LANES]

    has_other = jnp.where(core == 0, cut > 0, cut < slices - 1)
    other_first = lax.rem(jnp.where(core == 0, cut - CORES, cut + 1) + slices, slices)
    other_side = jnp.where(core == 0, 3, 0)
    n_owners = BLOCKS + jnp.where(has_other, BLOCKS, 0) - jnp.where(is_owner, 1, 0)
    pl.semaphore_wait(barrier, n_owners)

    def leaf_copy(b, turn):
        own = core != turn
        side = jnp.where(own, 1 + core, other_side)
        y, z, c = OWNERS[b]
        return pltpu.make_async_remote_copy(
            src_ref=send_buf.at[b],
            dst_ref=leaf_buf.at[side, slot_of(group)],
            send_sem=leaf_send,
            recv_sem=leaf_recv.at[side, late],
            device_id=(y * SIDE + z, jnp.where(own, first, other_first) + c),
            device_id_type=MESH,
        )

    for turn in range(2):
        valid = jnp.where(core != turn, True, has_other)

        @pl.when(jnp.logical_and(valid, jnp.logical_not(is_owner)))
        def _():
            for b in range(BLOCKS):
                leaf_copy(b, turn).start()

        @pl.when(jnp.logical_and(valid, is_owner))
        def _():
            for b in range(BLOCKS):

                @pl.when(jnp.logical_or(core == turn, mine != b))
                def _():
                    leaf_copy(b, turn).start()

    def all_left(count):
        sent = send_buf.at[pl.ds(0, count)]
        pltpu.make_async_copy(sent, sent, leaf_send).wait()

    pl.when(is_owner)(lambda: all_left(BLOCKS - 1))
    pl.when(jnp.logical_not(is_owner))(lambda: all_left(BLOCKS))
    pl.when(has_other)(lambda: all_left(BLOCKS))

    @pl.when(is_owner)
    def _():
        leaf_buf[1 + core, slot_of(group)] = send_buf[mine]
        row, col = iota((SIZE, SIZE), 0), iota((SIZE, SIZE), 1)
        place = lax.rem(col, HALF)
        z = (
            col // GROUPS * (SIDE // 2)
            + lax.rem(place // SIDE, QUARTER) * 2
            + place // (SIDE * QUARTER)
        )
        natural = 2 * (lax.rem(place, SIDE) * SIDE + z) + lax.rem(col // HALF, 2)
        order = (row == natural).astype(jnp.bfloat16)
        tree = tree_matrix(bank_ref, index_ref) * (1.0 / math.sqrt(views))
        served = (col == 2 * (lax.rem(row // 2, SIDE) * SIDE + row // (2 * SIDE)) + lax.rem(row, 2)).astype(jnp.bfloat16)
        high, low = [
            jnp.dot(
                served,
                jnp.dot(part, order, preferred_element_type=jnp.float32).astype(jnp.bfloat16),
                preferred_element_type=jnp.float32,
            ).astype(jnp.bfloat16)
            for part in parts_of(tree)
        ]
        for part in range(2):
            span = slice(part * GROUPS, (part + 1) * GROUPS)
            tree_buf[part] = jnp.concatenate([high[:, span], low[:, span], high[:, span]], axis=1)

        lane, place = iota((HALF, LANES), 1), iota((HALF, LANES), 0)

        def arrived(side, part):
            def wait(count):
                done = leaf_buf.at[side, pl.ds(0, count)]
                pltpu.make_async_copy(done, done, leaf_recv.at[side, part]).wait()

            if side in (1, 2) and part == 0:
                own = core == side - 1
                pl.when(own)(lambda: wait(HALF - 1))
                pl.when(jnp.logical_not(own))(lambda: wait(HALF))
            else:
                pl.when(has_side[side])(lambda: wait(HALF))

        def merged(part, terms):
            return jnp.dot(tree_buf[part], terms_of(part, terms), preferred_element_type=jnp.float32)

        def terms_of(part, terms):
            pair = lax.rem(place, SIDE) * (SIDE // 2) + lax.rem(place // SIDE, QUARTER) + part * QUARTER
            moved = [GROUPS // 4 - 1 - pair, pair - GROUPS // 4]
            back = lax.rem(lane - moved[0] + LANES // 2 + LANES, LANES)
            mixed = []
            for c in range(window):
                total = None
                for tap, side in terms:
                    value = taps_ref[tap] * leaf_buf[side, part * HALF : (part + 1) * HALF, c, :]
                    if side in (0, 3):
                        value = jnp.where(has_side[side], value, 0.0)
                    total = value if total is None else total + value
                mixed.append(total)
            rows = []
            for r in range(2):
                turned = []
                for c in range(window):
                    if r == 0:
                        turned.append(jnp.take_along_axis(mixed[c], back, axis=1))
                        continue
                    pieces = []
                    for k in range(HALF // SIDE):
                        base = LANES // 2 - GROUPS // 4 + part * QUARTER + k % QUARTER
                        piece = mixed[c][k * SIDE : (k + 1) * SIDE]
                        pieces.append(pltpu.roll(piece, base, 1, stride=SIDE // 2, stride_axis=0))
                    turned.append(jnp.concatenate(pieces, axis=0))
                rows.append(
                    jnp.concatenate(
                        [jnp.where(lane - moved[r] < LANES // 2, turned[i], turned[i + 1]) for i in range(per_block)],
                        axis=1,
                    )
                )
            high, low = parts_of(jnp.concatenate(rows, axis=0))
            return jnp.concatenate([high, high, low], axis=0)

        def keep(e, image, begin=0):
            for i in range(per_block):
                result_buf[e, begin : begin + image.shape[0], i, :] = image[:, i * LANES : (i + 1) * LANES]

        def give(e, step):
            turn = lax.rem(step, SIDE)
            y = jnp.where(turn < SIDE // 2, turn, SIDE + SIDE // 2 - 1 - turn)
            z = lax.div(step, SIDE)
            target = y * SIDE + z

            @pl.when(jnp.logical_or(target != group, core != e))
            def _():
                pltpu.make_async_remote_copy(
                    src_ref=result_buf.at[e, pl.ds(2 * (z * SIDE + y), 2)],
                    dst_ref=image_buf.at[pl.ds(2 * mine, 2)],
                    send_sem=image_send,
                    recv_sem=image_recv.at[mine],
                    device_id=(target, first + e),
                    device_id_type=MESH,
                ).start()

        def give_all(start, stop, which):
            def body(step, carry):
                for e in which:
                    give(e, step)
                return carry

            lax.fori_loop(start, stop, body, 0)

        for side in range(4):
            arrived(side, 0)
        early_buf[0] = merged(0, [(0, 0), (1, 1), (2, 2)])
        early_buf[1] = merged(0, [(0, 1), (1, 2), (2, 3)])
        for side in range(3):
            arrived(side, 1)
        keep(0, early_buf[0] + merged(1, [(0, 0), (1, 1), (2, 2)]))
        give_all(0, AHEAD, (0,))
        early_buf[1] += merged(1, [(0, 1), (1, 2)])
        arrived(3, 1)
        last = terms_of(1, [(2, 3)])
        for begin, end in ((0, 2 * SIDE), (2 * SIDE, SIZE)):
            keep(
                1,
                early_buf[1, begin:end]
                + jnp.dot(tree_buf[1, begin:end], last, preferred_element_type=jnp.float32),
                begin,
            )
            if begin == 0:
                give_all(0, SIDE, (1,))
        give_all(SIDE, AHEAD + LEAD, (1,))

        def give_both(step, carry):
            give(0, step)
            give(1, step + LEAD)
            return carry

        lax.fori_loop(AHEAD, GROUPS - LEAD, give_both, 0)
        give_all(GROUPS - LEAD, GROUPS, (0,))
        image_buf[pl.ds(2 * mine, 2)] = result_buf[core, pl.ds(2 * (lax.rem(group, SIDE) * SIDE + lax.div(group, SIDE)), 2)]

    for b in range(BLOCKS):
        got = image_buf.at[pl.ds(2 * b, 2)]

        @pl.when(jnp.logical_not(jnp.logical_and(is_owner, mine == b)))
        def _():
            pltpu.make_async_copy(got, got, image_recv.at[b]).wait()

        for i in range(per_block):
            c = b * per_block + i
            out_ref[:, c * LANES : (c + 1) * LANES] = image_buf[2 * b : 2 * b + 2, i, :]

    @pl.when(is_owner)
    def _():
        for e in range(CORES):
            own = core == e

            def wait(count):
                sent = result_buf.at[e, pl.ds(0, 2 * count)]
                pltpu.make_async_copy(sent, sent, image_send).wait()

            pl.when(own)(lambda: wait(GROUPS - 1))
            pl.when(jnp.logical_not(own))(lambda: wait(GROUPS))


def shards(sinogram, estimate, interp_bank, interp_index, slice_taps):
    _, views, columns = sinogram.shape
    per_block = columns // LANES // BLOCKS
    bank = jnp.swapaxes(interp_bank, 1, 2)
    operands = (sinogram[0], bank, interp_index.reshape(1, -1), slice_taps)
    held = [pltpu.with_memory_space_constraint(x, pltpu.HBM) for x in operands]
    mixed = pl.pallas_call(
        kernel,
        out_shape=pltpu.VMEM((2, columns), jnp.float32),
        in_specs=[pl.BlockSpec(memory_space=pltpu.HBM)] * 4,
        out_specs=pl.BlockSpec(memory_space=pltpu.VMEM),
        scratch_shapes=[
            pltpu.VMEM((views, columns), jnp.bfloat16),
            pltpu.VMEM(bank.shape, jnp.float32),
            pltpu.VMEM((1, SIZE), jnp.int32),
            pltpu.SMEM((3,), jnp.float32),
            pltpu.VMEM((BLOCKS, per_block + 1, LANES), jnp.float32),
            pltpu.VMEM((4, GROUPS, per_block + 1, LANES), jnp.float32),
            pltpu.VMEM((CORES, SIZE, per_block, LANES), jnp.float32),
            pltpu.VMEM((2 * BLOCKS, per_block, LANES), jnp.float32),
            pltpu.VMEM((2, SIZE, 3 * GROUPS), jnp.bfloat16),
            pltpu.VMEM((CORES, SIZE, columns // BLOCKS), jnp.float32),
            pltpu.SemaphoreType.DMA((4,)),
            pltpu.SemaphoreType.DMA,
            pltpu.SemaphoreType.DMA((4, 2)),
            pltpu.SemaphoreType.DMA,
            pltpu.SemaphoreType.DMA((BLOCKS,)),
        ],
        compiler_params=pltpu.CompilerParams(
            collective_id=0, has_side_effects=True, vmem_limit_bytes=32 * 1024 * 1024
        ),
    )(*held)
    return (estimate[0].astype(jnp.float32) - mixed)[None]


def solution(mesh):
    in_specs = (P("cuts", "angle", None), P("cuts", "angle", None), P(), P(), P())
    out_specs = P("cuts", "angle", None)
    return jax.shard_map(shards, mesh=mesh, in_specs=in_specs, out_specs=out_specs, check_vma=False)
```

```python
import functools
import math

import jax
import jax.numpy as jnp
from jax import lax
from jax.experimental import pallas as pl
from jax.experimental.pallas import tpu as pltpu
from jax.sharding import PartitionSpec as P

MESH = pl.DeviceIdType.MESH
SIDE = 8
CORES = 2
LANES = 128
GROUPS = SIDE * SIDE
SIZE = 2 * GROUPS
OWNERS = ((0, 1, 0), (0, 1, 1), (1, 1, 0), (1, 1, 1), (4, 0, 0), (1, 0, 0), (2, 0, 0), (2, 0, 1), (7, 0, 0), (7, 0, 1), (6, 0, 0), (6, 0, 1), (3, 0, 0), (3, 0, 1), (5, 0, 0), (5, 0, 1))
BLOCKS = len(OWNERS)
AHEAD, LEAD = 10, 2
QUARTER = SIDE // 4
HALF = GROUPS // 2


def parts_of(value):
    high = value.astype(jnp.bfloat16)
    low = (value - high.astype(jnp.float32)).astype(jnp.bfloat16)
    return high, low


def iota(shape, dim):
    return lax.broadcasted_iota(jnp.int32, shape, dim)


def tree_matrix(bank_ref, index_ref):
    kinds, half = bank_ref.shape[:2]
    levels = GROUPS.bit_length() - 1
    index = jnp.broadcast_to(index_ref[...].astype(jnp.float32), (8, SIZE))
    product = None
    for level in range(1, levels + 1):
        width = SIZE >> level
        row, col = iota((SIZE, SIZE), 0), iota((SIZE, SIZE), 1)
        chosen = (row == (1 << level) + col // width).astype(jnp.float32)
        kind = jnp.dot(index, chosen, preferred_element_type=jnp.float32)[0:1]
        block = jnp.zeros((2 * width, SIZE), jnp.float32)
        pick = iota((half, SIZE), 0) == iota((half, SIZE), 1) % width
        for k in range(kinds):
            place = jnp.where(pick & (jnp.abs(kind - k) < 0.5), 1.0, 0.0)
            block += lax.dot_general(
                bank_ref[k, :, :],
                place,
                (((0,), (0,)), ((), ())),
                precision=lax.Precision.HIGHEST,
                preferred_element_type=jnp.float32,
            )[: 2 * width]
        if 2 * width < 8:
            block = jnp.concatenate([block] * (8 // (2 * width)), axis=0)
        factor = jnp.concatenate([block] * (SIZE // block.shape[0]), axis=0)
        factor = jnp.where(row // (2 * width) == col // (2 * width), factor, 0.0)
        if product is None:
            product = factor
        else:
            product = jnp.dot(
                product, factor, precision=lax.Precision.HIGHEST, preferred_element_type=jnp.float32
            )
    return product


def far_first(turn):
    back = lax.rem(turn, 2)
    return SIDE // 2 + (1 - 2 * back) * lax.div(turn + back, 2)


def slot_of(group):
    y, z = lax.div(group, SIDE), lax.rem(group, SIDE)
    late, rest = lax.div(z, SIDE // 2), lax.rem(z, SIDE // 2)
    return ((late * 2 + lax.rem(rest, 2)) * QUARTER + lax.div(rest, 2)) * SIDE + y


def kernel(
    sino_any, bank_any, index_any, taps_any, out_ref,
    sino_ref, bank_ref, index_ref, taps_ref, send_buf, leaf_buf, result_buf, image_buf, tree_buf, early_buf,
    local_sem, leaf_send, leaf_recv, image_send, image_recv,
):
    views, columns = sino_ref.shape
    per_block = columns // LANES // BLOCKS
    window = per_block + 1
    slices = lax.axis_size("cuts")
    group = lax.axis_index("angle")
    cut = lax.axis_index("cuts")
    core = lax.rem(cut, CORES)
    first = cut - core
    here = [jnp.logical_and(group == y * SIDE + z, core == c) for y, z, c in OWNERS]
    is_owner = functools.reduce(jnp.logical_or, here)
    mine = sum(jnp.where(hit, b, 0) for b, hit in enumerate(here))
    late = lax.div(lax.rem(group, SIDE), SIDE // 2)

    has_side = [first > 0, True, True, first + CORES < slices]
    side_cut = [lax.rem(first + side - 1 + slices, slices) for side in range(4)]

    barrier = pltpu.get_barrier_semaphore()
    sino_copy = pltpu.make_async_copy(sino_any, sino_ref, local_sem.at[0])
    sino_copy.start()

    @pl.when(is_owner)
    def _():
        bank_copy = pltpu.make_async_copy(bank_any, bank_ref, local_sem.at[1])
        index_copy = pltpu.make_async_copy(index_any, index_ref, local_sem.at[2])
        taps_copy = pltpu.make_async_copy(taps_any, taps_ref, local_sem.at[3])
        bank_copy.start()
        index_copy.start()
        taps_copy.start()

        def announce(step, carry):
            y = lax.rem(lax.div(group, SIDE) + far_first(lax.rem(step, SIDE)), SIDE)
            z = lax.rem(group + far_first(lax.div(step, SIDE)), SIDE)
            target = y * SIDE + z
            for side in range(4):
                valid = has_side[side]
                if side in (1, 2):
                    valid = jnp.logical_or(target != group, core != side - 1)

                @pl.when(valid)
                def _():
                    pl.semaphore_signal(barrier, inc=1, device_id=(target, side_cut[side]), device_id_type=MESH)

            return carry

        lax.fori_loop(0, GROUPS, announce, 0)
        bank_copy.wait()
        index_copy.wait()
        taps_copy.wait()

    has_other = jnp.where(core == 0, cut > 0, cut < slices - 1)
    other_first = lax.rem(jnp.where(core == 0, cut - CORES, cut + 1) + slices, slices)
    other_side = jnp.where(core == 0, 3, 0)
    n_owners = BLOCKS + jnp.where(has_other, BLOCKS, 0) - jnp.where(is_owner, 1, 0)
    pl.semaphore_wait(barrier, n_owners)

    def leaf_copy(b, turn):
        own = core != turn
        side = jnp.where(own, 1 + core, other_side)
        y, z, c = OWNERS[b]
        return pltpu.make_async_remote_copy(
            src_ref=send_buf.at[b],
            dst_ref=leaf_buf.at[side, slot_of(group)],
            send_sem=leaf_send,
            recv_sem=leaf_recv.at[side, late],
            device_id=(y * SIDE + z, jnp.where(own, first, other_first) + c),
            device_id_type=MESH,
        )

    sino_copy.wait()
    total = jnp.sum(sino_ref[...].astype(jnp.float32), axis=0, keepdims=True)
    margin = jnp.zeros((1, LANES // 2), jnp.float32)
    total = jnp.concatenate([margin, total, margin], axis=1)
    for b in range(BLOCKS):
        for c in range(window):
            start = (b * per_block + c) * LANES
            send_buf[b, c : c + 1, :] = total[:, start : start + LANES]

    for turn in range(2):
        valid = jnp.where(core != turn, True, has_other)

        @pl.when(jnp.logical_and(valid, jnp.logical_not(is_owner)))
        def _():
            for b in range(BLOCKS):
                leaf_copy(b, turn).start()

        @pl.when(jnp.logical_and(valid, is_owner))
        def _():
            for b in range(BLOCKS):

                @pl.when(jnp.logical_or(core == turn, mine != b))
                def _():
                    leaf_copy(b, turn).start()

    def all_left(count):
        sent = send_buf.at[pl.ds(0, count)]
        pltpu.make_async_copy(sent, sent, leaf_send).wait()

    pl.when(is_owner)(lambda: all_left(BLOCKS - 1))
    pl.when(jnp.logical_not(is_owner))(lambda: all_left(BLOCKS))
    pl.when(has_other)(lambda: all_left(BLOCKS))

    @pl.when(is_owner)
    def _():
        leaf_buf[1 + core, slot_of(group)] = send_buf[mine]
        row, col = iota((SIZE, SIZE), 0), iota((SIZE, SIZE), 1)
        place = lax.rem(col, HALF)
        z = (
            col // GROUPS * (SIDE // 2)
            + lax.rem(place // SIDE, QUARTER) * 2
            + place // (SIDE * QUARTER)
        )
        natural = 2 * (lax.rem(place, SIDE) * SIDE + z) + lax.rem(col // HALF, 2)
        order = (row == natural).astype(jnp.bfloat16)
        tree = tree_matrix(bank_ref, index_ref) * (1.0 / math.sqrt(views))
        served = (col == 2 * (lax.rem(row // 2, SIDE) * SIDE + row // (2 * SIDE)) + lax.rem(row, 2)).astype(jnp.bfloat16)
        high, low = [
            jnp.dot(
                served,
                jnp.dot(part, order, preferred_element_type=jnp.float32).astype(jnp.bfloat16),
                preferred_element_type=jnp.float32,
            ).astype(jnp.bfloat16)
            for part in parts_of(tree)
        ]
        for part in range(2):
            span = slice(part * GROUPS, (part + 1) * GROUPS)
            tree_buf[part] = jnp.concatenate([high[:, span], low[:, span], high[:, span]], axis=1)

        lane, place = iota((HALF, LANES), 1), iota((HALF, LANES), 0)

        def arrived(side, part):
            def wait(count):
                done = leaf_buf.at[side, pl.ds(0, count)]
                pltpu.make_async_copy(done, done, leaf_recv.at[side, part]).wait()

            if side in (1, 2) and part == 0:
                own = core == side - 1
                pl.when(own)(lambda: wait(HALF - 1))
                pl.when(jnp.logical_not(own))(lambda: wait(HALF))
            else:
                pl.when(has_side[side])(lambda: wait(HALF))

        def merged(part, terms):
            return jnp.dot(tree_buf[part], terms_of(part, terms), preferred_element_type=jnp.float32)

        def terms_of(part, terms):
            pair = lax.rem(place, SIDE) * (SIDE // 2) + lax.rem(place // SIDE, QUARTER) + part * QUARTER
            moved = [GROUPS // 4 - 1 - pair, pair - GROUPS // 4]
            back = lax.rem(lane - moved[0] + LANES // 2 + LANES, LANES)
            mixed = []
            for c in range(window):
                total = None
                for tap, side in terms:
                    value = taps_ref[tap] * leaf_buf[side, part * HALF : (part + 1) * HALF, c, :]
                    if side in (0, 3):
                        value = jnp.where(has_side[side], value, 0.0)
                    total = value if total is None else total + value
                mixed.append(total)
            rows = []
            for r in range(2):
                turned = []
                for c in range(window):
                    if r == 0:
                        turned.append(jnp.take_along_axis(mixed[c], back, axis=1))
                        continue
                    pieces = []
                    for k in range(HALF // SIDE):
                        base = LANES // 2 - GROUPS // 4 + part * QUARTER + k % QUARTER
                        piece = mixed[c][k * SIDE : (k + 1) * SIDE]
                        pieces.append(pltpu.roll(piece, base, 1, stride=SIDE // 2, stride_axis=0))
                    turned.append(jnp.concatenate(pieces, axis=0))
                rows.append(
                    jnp.concatenate(
                        [jnp.where(lane - moved[r] < LANES // 2, turned[i], turned[i + 1]) for i in range(per_block)],
                        axis=1,
                    )
                )
            high, low = parts_of(jnp.concatenate(rows, axis=0))
            return jnp.concatenate([high, high, low], axis=0)

        def keep(e, image, begin=0):
            for i in range(per_block):
                result_buf[e, begin : begin + image.shape[0], i, :] = image[:, i * LANES : (i + 1) * LANES]

        def give(e, step):
            turn = lax.rem(step, SIDE)
            y = jnp.where(turn < SIDE // 2, turn, SIDE + SIDE // 2 - 1 - turn)
            z = lax.div(step, SIDE)
            target = y * SIDE + z

            @pl.when(jnp.logical_or(target != group, core != e))
            def _():
                pltpu.make_async_remote_copy(
                    src_ref=result_buf.at[e, pl.ds(2 * (z * SIDE + y), 2)],
                    dst_ref=image_buf.at[pl.ds(2 * mine, 2)],
                    send_sem=image_send,
                    recv_sem=image_recv.at[mine],
                    device_id=(target, first + e),
                    device_id_type=MESH,
                ).start()

        def give_all(start, stop, which):
            def body(step, carry):
                for e in which:
                    give(e, step)
                return carry

            lax.fori_loop(start, stop, body, 0)

        for side in range(4):
            arrived(side, 0)
        early_buf[0] = merged(0, [(0, 0), (1, 1), (2, 2)])
        early_buf[1] = merged(0, [(0, 1), (1, 2), (2, 3)])
        for side in range(3):
            arrived(side, 1)
        keep(0, early_buf[0] + merged(1, [(0, 0), (1, 1), (2, 2)]))
        give_all(0, AHEAD, (0,))
        early_buf[1] += merged(1, [(0, 1), (1, 2)])
        arrived(3, 1)
        last = terms_of(1, [(2, 3)])
        for begin, end in ((0, 2 * SIDE), (2 * SIDE, SIZE)):
            keep(
                1,
                early_buf[1, begin:end]
                + jnp.dot(tree_buf[1, begin:end], last, preferred_element_type=jnp.float32),
                begin,
            )
            if begin == 0:
                give_all(0, SIDE, (1,))
        give_all(SIDE, AHEAD + LEAD, (1,))

        def give_both(step, carry):
            give(0, step)
            give(1, step + LEAD)
            return carry

        lax.fori_loop(AHEAD, GROUPS - LEAD, give_both, 0)
        give_all(GROUPS - LEAD, GROUPS, (0,))
        image_buf[pl.ds(2 * mine, 2)] = result_buf[core, pl.ds(2 * (lax.rem(group, SIDE) * SIDE + lax.div(group, SIDE)), 2)]

    for b in range(BLOCKS):
        got = image_buf.at[pl.ds(2 * b, 2)]

        @pl.when(jnp.logical_not(jnp.logical_and(is_owner, mine == b)))
        def _():
            pltpu.make_async_copy(got, got, image_recv.at[b]).wait()

        for i in range(per_block):
            c = b * per_block + i
            out_ref[:, c * LANES : (c + 1) * LANES] = image_buf[2 * b : 2 * b + 2, i, :]

    @pl.when(is_owner)
    def _():
        for e in range(CORES):
            own = core == e

            def wait(count):
                sent = result_buf.at[e, pl.ds(0, 2 * count)]
                pltpu.make_async_copy(sent, sent, image_send).wait()

            pl.when(own)(lambda: wait(GROUPS - 1))
            pl.when(jnp.logical_not(own))(lambda: wait(GROUPS))


def shards(sinogram, estimate, interp_bank, interp_index, slice_taps):
    _, views, columns = sinogram.shape
    per_block = columns // LANES // BLOCKS
    bank = jnp.swapaxes(interp_bank, 1, 2)
    operands = (sinogram[0], bank, interp_index.reshape(1, -1), slice_taps)
    held = [pltpu.with_memory_space_constraint(x, pltpu.HBM) for x in operands]
    mixed = pl.pallas_call(
        kernel,
        out_shape=pltpu.VMEM((2, columns), jnp.float32),
        in_specs=[pl.BlockSpec(memory_space=pltpu.HBM)] * 4,
        out_specs=pl.BlockSpec(memory_space=pltpu.VMEM),
        scratch_shapes=[
            pltpu.VMEM((views, columns), jnp.bfloat16),
            pltpu.VMEM(bank.shape, jnp.float32),
            pltpu.VMEM((1, SIZE), jnp.int32),
            pltpu.SMEM((3,), jnp.float32),
            pltpu.VMEM((BLOCKS, per_block + 1, LANES), jnp.float32),
            pltpu.VMEM((4, GROUPS, per_block + 1, LANES), jnp.float32),
            pltpu.VMEM((CORES, SIZE, per_block, LANES), jnp.float32),
            pltpu.VMEM((2 * BLOCKS, per_block, LANES), jnp.float32),
            pltpu.VMEM((2, SIZE, 3 * GROUPS), jnp.bfloat16),
            pltpu.VMEM((CORES, SIZE, columns // BLOCKS), jnp.float32),
            pltpu.SemaphoreType.DMA((4,)),
            pltpu.SemaphoreType.DMA,
            pltpu.SemaphoreType.DMA((4, 2)),
            pltpu.SemaphoreType.DMA,
            pltpu.SemaphoreType.DMA((BLOCKS,)),
        ],
        compiler_params=pltpu.CompilerParams(
            collective_id=0, has_side_effects=True, vmem_limit_bytes=32 * 1024 * 1024
        ),
    )(*held)
    return (estimate[0].astype(jnp.float32) - mixed)[None]


def solution(mesh):
    in_specs = (P("cuts", "angle", None), P("cuts", "angle", None), P(), P(), P())
    out_specs = P("cuts", "angle", None)
    return jax.shard_map(shards, mesh=mesh, in_specs=in_specs, out_specs=out_specs, check_vma=False)
```
